32 devices in a mesh: head: 4 (over z), page: 8 (over y, x, core).
Axes of the slice: x: 2, y: 2, z: 4, core: 2. Of those that a mesh axis runs over, the one named last changes fastest.
Arguments:
- doc_states: bfloat16 [512, 2048], P('page'), may hold values from -6 to 6
- gain_attn: float32 [2048], replicated, may hold values from 0.1 to 1.9
- query_weight: bfloat16 [2048, 2048], P(None, 'head'), may hold values from -0.125 to 0.125
- cache_keys: bfloat16 [16, 128, 2048], P('page', None, 'head'), may hold values from -144 to 144
- cache_values: bfloat16 [16, 128, 2048], P('page', None, 'head'), may hold values from -6 to 6
- rel_bucket: int32 [16, 128], P('page'), may hold values from 0 to 31
- bias_table: float32 [32, 32], P(None, 'head'), may hold values from -4 to 4
- out_weight: bfloat16 [2048, 2048], P('head'), may hold values from -0.125 to 0.125
- gain_ffn: float32 [2048], replicated, may hold values from 0.1 to 1.9
- wi_gate: bfloat16 [2048, 5120], P(None, 'head'), may hold values from -0.125 to 0.125
- wi_up: bfloat16 [2048, 5120], P(None, 'head'), may hold values from -0.125 to 0.125
- wo_ffn: bfloat16 [5120, 2048], P('head'), may hold values from -0.078125 to 0.078125
- score_vector: float32 [2048], replicated, may hold values from -0.125 to 0.125
- query_lengths: int32 [8], replicated, may hold values from 1 to 256
- doc_query: int32 [64], replicated, may hold values from 0 to 7
- doc_of_token: int32 [512], replicated, may hold values from 0 to 63, as said below
- page_table: int32 [16], replicated, may hold values from 0 to 15, each once
Outputs:
- doc_scores: float32 [64], P('page')
The draws below stay inside these ranges and needn't reach their ends.
Inputs may be any that keep to these rules, and one draw needn't show every extreme that they name: page_table lists every physical page once. `doc_of_token`: the tokens of each document form one contiguous run of 1 to 256 tokens; every document has one run, and some document has exactly 256 tokens.
All inputs are finite; a program needn't handle non-finite values.
Results may differ from the reference program's by a relative error of at most 0.03.
Values may be sent and summed in bfloat16 or wider, within the bound.
A program may use at most 320 MiB of HBM per device.

```python
import jax
import jax.numpy as jnp
from jax import lax

D = 2048
H = 32
DH = 64
FF = 5120
NB = 32
PAGE_LEN = 128
NQ = 8
TOK_DEV = 64
TOKENS = 512
PAGES = 16
MAXP = 2
NDOC = 64
MOST_DOC = 256


def draw_cache_keys(key, part):
    order = jax.random.permutation(jax.random.fold_in(key, 11), H)
    factor = jnp.where(order == 0, 80.0, jnp.where(order == 1, 40.0, jnp.where(order == 2, 16.0, 1.0)))
    column = jnp.repeat(factor, DH)
    entries = jax.random.fold_in(key, 12)
    shape = (PAGES, PAGE_LEN, H * DH)
    base = jnp.clip(jax.random.normal(entries, shape, jnp.float32), -6.0, 6.0)
    return (0.3 * base * column[None, None, :]).astype(jnp.bfloat16)


def draw_doc_of_token(key, part):
    middle = NDOC - 2
    remain = TOKENS - TOK_DEV - MOST_DOC
    stride = remain // middle
    index = jnp.arange(middle + 1, dtype=jnp.int32)
    jitter = jax.random.randint(jax.random.fold_in(key, 21), (middle + 1,), 0, stride, dtype=jnp.int32)
    jitter = jnp.where((index == 0) | (index == middle), 0, jitter)
    cuts = index * remain // middle + jitter
    starts = jnp.concatenate([jnp.array([0, TOK_DEV], jnp.int32), (TOK_DEV + MOST_DOC + cuts[:-1]).astype(jnp.int32)])
    positions = jnp.arange(TOKENS, dtype=jnp.int32)
    segment = jnp.sum((positions[:, None] >= starts[None, 1:]).astype(jnp.int32), axis=1).astype(jnp.int32)
    order = jax.random.permutation(jax.random.fold_in(key, 22), NDOC).astype(jnp.int32)
    pinned = NDOC // 2
    order = jnp.where(order == pinned, order[0], order)
    order = order.at[0].set(pinned)
    return order[segment].astype(jnp.int32)


def plant(values, rng, least, high):
    longest = values.shape.index(max(values.shape))
    spots = []
    for shift in (0, 1):
        where = [jax.random.randint(jax.random.fold_in(rng, axis), (), 0, length) for axis, length in enumerate(values.shape)]
        where[longest] = (where[longest] + shift) % values.shape[longest]
        spots.append(tuple(where))
    return values.at[spots[0]].set(least).at[spots[1]].set(high)


def block_scale(rng, dims, split, smallest, largest):
    level = 1.0
    for dim, parts in split:
        heights = jax.random.uniform(jax.random.fold_in(jax.random.fold_in(rng, 6), dim), (parts,), jnp.float32, smallest / len(split), largest / len(split))
        level = level * jnp.repeat(jnp.exp(heights), dims[dim] // parts).reshape((-1,) + (1,) * (len(dims) - 1 - dim))
    return level


def noise(own_key, extent, spread, bound, split=(), kind=jnp.bfloat16):
    values = jax.random.normal(own_key, extent, jnp.float32) * spread
    if len(split) > 0:
        values = block_scale(own_key, extent, split, -0.22, 0.18) * values
    return jnp.clip(values, min=-bound, max=bound).astype(kind)


def setup_inputs(seed: int = 0) -> dict:
    key_list = jax.random.split(jax.random.key(seed), 18)
    return {
        "doc_states": noise(key_list[0], (TOKENS, D), 1.0, 6.0, ((0, 8),)),
        "gain_attn": jnp.clip(1.0 + 0.18 * jax.random.normal(key_list[1], (D,), jnp.float32), 0.1, 1.9),
        "query_weight": noise(key_list[2], (D, H * DH), D ** -0.5, 0.125, ((1, 4),)),
        "cache_keys": draw_cache_keys(jax.random.fold_in(key_list[17], 71), 0),
        "cache_values": noise(key_list[4], (PAGES, PAGE_LEN, H * DH), 1.0, 6.0, ((0, 8), (2, 4))),
        "rel_bucket": plant(jax.random.randint(key_list[5], (PAGES, PAGE_LEN), 0, NB), jax.random.fold_in(key_list[5], 1), 0, NB - 1).astype(jnp.int32),
        "bias_table": noise(key_list[6], (NB, H), 1.0, 4.0, ((1, 4),), jnp.float32),
        "out_weight": noise(key_list[7], (H * DH, D), (H * DH) ** -0.5, 0.125, ((0, 4),)),
        "gain_ffn": jnp.clip(1.0 + 0.18 * jax.random.normal(key_list[8], (D,), jnp.float32), 0.1, 1.9),
        "wi_gate": noise(key_list[9], (D, FF), D ** -0.5, 0.125, ((1, 4),)),
        "wi_up": noise(key_list[10], (D, FF), D ** -0.5, 0.125, ((1, 4),)),
        "wo_ffn": noise(key_list[11], (FF, D), FF ** -0.5, 0.078125, ((0, 4),)),
        "score_vector": noise(key_list[12], (D,), D ** -0.5, 0.125, (), jnp.float32),
        "query_lengths": plant(jax.random.randint(key_list[13], (NQ,), 1, MAXP * PAGE_LEN + 1), jax.random.fold_in(key_list[13], 1), 1, MAXP * PAGE_LEN).astype(jnp.int32),
        "doc_query": plant(jax.random.randint(key_list[14], (NDOC,), 0, NQ), jax.random.fold_in(key_list[14], 1), 0, NQ - 1).astype(jnp.int32),
        "doc_of_token": draw_doc_of_token(jax.random.fold_in(key_list[17], 71), 0),
        "page_table": jax.random.permutation(key_list[16], PAGES).astype(jnp.int32),
    }


def rms_scale(values, gain):
    values = values.astype(jnp.float32)
    return values * lax.rsqrt(lax.optimization_barrier(jnp.mean(values * values, axis=-1, keepdims=True)) + 1e-06) * gain

def reference(doc_states, gain_attn, query_weight, cache_keys, cache_values, rel_bucket, bias_table, out_weight, gain_ffn, wi_gate, wi_up, wo_ffn, score_vector, query_lengths, doc_query, doc_of_token, page_table):
    width = H * DH
    span = MAXP * PAGE_LEN
    normed = rms_scale(doc_states, gain_attn).astype(jnp.bfloat16)
    queries = jnp.dot(normed, query_weight, preferred_element_type=jnp.float32).astype(jnp.bfloat16)
    tok_query = doc_query[doc_of_token].astype(jnp.int32)
    table = page_table.reshape(NQ, MAXP)
    keys_all = cache_keys[table].reshape(NQ, span, H, DH).astype(jnp.float32)
    values_all = cache_values[table].reshape(NQ, span, H, DH).astype(jnp.float32)
    bias_all = jnp.transpose(bias_table[rel_bucket[table].reshape(NQ, span)], (0, 2, 1))
    valid_all = jnp.arange(span)[None, :] < query_lengths[:, None]
    block = min(512, TOKENS)
    count = TOKENS // block

    def one_block(pair):
        rows, owners = pair
        heads = rows.reshape(block, H, DH).astype(jnp.float32)

        def per_query(carry, index):
            scores = jnp.einsum('rhd,khd->rhk', heads, keys_all[index], precision=lax.Precision.HIGHEST) + bias_all[index][None]
            mask = valid_all[index][None, None, :]
            top = lax.optimization_barrier(jnp.max(jnp.where(mask, scores, -1e+30), axis=-1))
            weights = jnp.where(mask, jnp.exp(scores - top[..., None]), 0.0)
            total = lax.optimization_barrier(jnp.sum(weights, axis=-1))
            rounded = weights.astype(jnp.bfloat16).astype(jnp.float32)
            summed = jnp.einsum('rhk,khd->rhd', rounded, values_all[index], precision=lax.Precision.HIGHEST)
            chosen = (owners == index)[:, None, None]
            context = jnp.where(chosen, summed / jnp.where(chosen[:, :, 0], total, 1.0)[..., None], carry)
            return (context, None)
        start = jnp.zeros((block, H, DH), jnp.float32)
        result, unused = lax.scan(per_query, start, jnp.arange(NQ, dtype=jnp.int32))
        return result.reshape(block, width).astype(jnp.bfloat16)
    context = lax.map(one_block, (queries.reshape(count, block, width), tok_query.reshape(count, block))).reshape(TOKENS, width)
    hidden = doc_states.astype(jnp.float32) + jnp.dot(context, out_weight, preferred_element_type=jnp.float32)
    normed_two = rms_scale(hidden, gain_ffn).astype(jnp.bfloat16)
    gate = jnp.dot(normed_two, wi_gate, preferred_element_type=jnp.float32)
    upper = jnp.dot(normed_two, wi_up, preferred_element_type=jnp.float32)
    middle = (jax.nn.gelu(gate, approximate=True) * upper).astype(jnp.bfloat16)
    final = hidden + jnp.dot(middle, wo_ffn, preferred_element_type=jnp.float32)
    tok_score = jnp.dot(final, score_vector, precision=lax.Precision.HIGHEST)
    sums = jax.ops.segment_sum(tok_score, doc_of_token, num_segments=NDOC)
    counts = jax.ops.segment_sum(jnp.ones((TOKENS,), jnp.float32), doc_of_token, num_segments=NDOC)
    return sums / counts
```

```python
import functools

import jax
import jax.numpy as jnp
from jax import lax
from jax.experimental import pallas as pl
from jax.experimental.pallas import tpu as pltpu
from jax.sharding import PartitionSpec as P

NQ = 8
FAR = -1e30
MESH = pl.DeviceIdType.MESH
F32 = jnp.float32
BF16 = jnp.bfloat16


def iota(shape, dim):
    return lax.broadcasted_iota(jnp.int32, shape, dim)


def dot(a, b):
    return jnp.dot(a, b, preferred_element_type=F32)


def dot_last(a, b):
    return lax.dot_general(a, b, (((1,), (1,)), ((), ())), preferred_element_type=F32)


def three_parts(value):
    first = value.astype(BF16).astype(F32)
    second = (value - first).astype(BF16).astype(F32)
    third = (value - first - second).astype(BF16).astype(F32)
    return first, second, third


def kernel(
    nz, npg,
    doc_hbm, ga, qw_hbm, ck_hbm, cv_hbm, rb, bt, ow_hbm, gf, wg_hbm, wu_hbm, wo_hbm, sv,
    ql, dq, dtok, pt,
    out,
    doc, qw, kbuf, vbuf, rbx, ow, wg, wu, wo, kz, vz, kbias, tokq_row, keyq_row,
    q_all, ax_out, ax, rs_out, rs, ag, fz, fp, w2,
    lsem, pair_s, pair_r, q_s, q_r, a_s, a_r, r_s, r_r, g_s, g_r, z_s, z_r, p_s, p_r,
):
    nc = npg // 2
    z = lax.axis_index("head")
    p = lax.axis_index("page")
    core = p % 2
    chip = p // 2
    partner = p + 1 - 2 * core
    toks, model = doc.shape
    width = qw.shape[1]
    heads = bt.shape[1]
    depth = width // heads
    pages, page_len = rb.shape
    span = 2 * pages * page_len
    total_toks = dtok.shape[1]
    ndoc = dq.shape[0]
    doc_dev = ndoc // npg
    block = model // nz
    all_pages = pt.shape[0]
    max_pages = all_pages // NQ

    barrier = pltpu.get_barrier_semaphore()
    for k in range(1, npg):
        pl.semaphore_signal(barrier, inc=1, device_id=(z, (p + k) % npg), device_id_type=MESH)
    for k in range(1, nz):
        pl.semaphore_signal(barrier, inc=1, device_id=((z + k) % nz, p), device_id_type=MESH)

    moves = []
    for n, (src, dst) in enumerate([
        (doc_hbm, doc), (qw_hbm, qw), (ck_hbm, kbuf.at[0]), (cv_hbm, vbuf.at[0]),
        (ow_hbm, ow), (wo_hbm, wo), (wg_hbm, wg), (wu_hbm, wu),
    ]):
        move = pltpu.make_async_copy(src, dst, lsem.at[n])
        move.start()
        moves.append(move)
    doc_in, qw_in, k_in, v_in, ow_in, wo_in, wg_in, wu_in = moves

    pl.semaphore_wait(barrier, npg - 1 + nz - 1)
    pairs = []
    for n, (src, dst) in enumerate([(ck_hbm, kbuf.at[1]), (cv_hbm, vbuf.at[1]), (rb, rbx)]):
        copy = pltpu.make_async_remote_copy(
            src_ref=src, dst_ref=dst, send_sem=pair_s.at[n], recv_sem=pair_r.at[n],
            device_id=(z, partner), device_id_type=MESH,
        )
        copy.start()
        pairs.append(copy)

    doc_in.wait()
    x = doc[...].astype(F32)
    scale = lax.rsqrt(jnp.mean(x * x, axis=1, keepdims=True) + 1e-6)
    normed = (x * scale * ga[...]).astype(BF16)
    qw_in.wait()
    q_all[0] = dot(normed, qw[...]).astype(BF16)

    def query_copy(k):
        return pltpu.make_async_remote_copy(
            src_ref=q_all.at[0], dst_ref=q_all.at[k], send_sem=q_s.at[k], recv_sem=q_r.at[k],
            device_id=(z, ((chip + k) % nc) * 2 + core), device_id_type=MESH,
        )

    for k in range(1, nc):
        query_copy(k).start()

    docs = dtok[...]

    def fill(d, carry):
        return jnp.where(docs == d, dq[d].astype(F32), carry)

    tokq_row[...] = lax.fori_loop(0, ndoc, fill, jnp.zeros((1, total_toks), F32))
    lane = iota((1, span), 1)
    half = span // 2
    page = jnp.where(lane < half, p * pages + lane // page_len, partner * pages + (lane - half) // page_len)
    owner = jnp.full((1, span), -1.0, F32)
    left = jnp.zeros((1, span), jnp.int32)
    for s in range(all_pages):
        hit = page == pt[s]
        owner = jnp.where(hit, float(s // max_pages), owner)
        left = jnp.where(hit, ql[s // max_pages] - (s % max_pages) * page_len, left)
    keyq_row[...] = jnp.where(lane % page_len < left, owner, -1.0)

    side = iota((1, 128), 1) // depth
    side_mask = [(side == s).astype(F32).astype(BF16) for s in range(128 // depth)]
    per = 128 // depth

    def split_heads(buf, dest, slot):
        for j in range(pages):
            rows = pl.ds((slot * pages + j) * page_len, page_len)
            for h in range(heads):
                g = h // per
                dest[h, rows, :] = buf[slot, j, :, g * 128:(g + 1) * 128] * side_mask[h % per]

    buckets = bt.shape[0]

    def bias_of(ref, slot):
        for j in range(pages):
            onehot = (ref[j:j + 1, :] == iota((buckets, page_len), 0)).astype(F32)
            part = lax.dot_general(
                bt[...], onehot, (((0,), (0,)), ((), ())),
                precision=lax.Precision.HIGHEST, preferred_element_type=F32,
            )
            at = (slot * pages + j) * page_len
            kbias[:, at:at + page_len] = part

    bias_of(rb, 0)
    k_in.wait()
    split_heads(kbuf, kz, 0)
    v_in.wait()
    split_heads(vbuf, vz, 0)
    for copy in pairs:
        copy.wait_recv()
    bias_of(rbx, 1)
    split_heads(kbuf, kz, 1)
    split_heads(vbuf, vz, 1)

    spot = iota((1, 128), 1)

    def token_column(row, first):
        hit = iota((toks, total_toks), 1) == iota((toks, total_toks), 0) + first
        return jnp.sum(jnp.where(hit, row, 0.0), axis=1, keepdims=True)

    def attend(k, dest):
        source = ((chip - k + nc) % nc) * 2 + core
        column = token_column(tokq_row[...], source * toks)
        far = jnp.where(column == keyq_row[...], 0.0, FAR)
        stats = jnp.zeros((toks, 128), F32)
        for g in range(width // 128):
            rows = q_all[k, :, g * 128:(g + 1) * 128]
            summed = jnp.zeros((toks, 128), F32)
            for h in range(g * per, (g + 1) * per):
                scores = dot_last(rows, kz[h]) + (far + kbias[h:h + 1, :])
                top = jnp.max(scores, axis=1, keepdims=True)
                weights = jnp.exp(scores - top)
                total = jnp.sum(weights, axis=1, keepdims=True)
                summed += dot(weights.astype(BF16), vz[h])
                stats = jnp.where((spot % heads == h) & (spot < 3 * heads), top, stats)
                stats = jnp.where((spot % heads == h) & (spot >= 3 * heads), total, stats)
            dest[:, g * 128:(g + 1) * 128] = summed.astype(BF16)
        a, b, c = three_parts(stats)
        part = (spot // heads) % 3
        packed = jnp.where(part == 0, a, jnp.where(part == 1, b, c))
        dest[:, width:] = jnp.where(spot < 6 * heads, packed, 0.0).astype(BF16)

    def partial_copy(k):
        return pltpu.make_async_remote_copy(
            src_ref=ax_out.at[k], dst_ref=ax.at[k], send_sem=a_s.at[k], recv_sem=a_r.at[k],
            device_id=(z, ((chip - k + nc) % nc) * 2 + core), device_id_type=MESH,
        )

    attend(0, ax.at[0])

    def serve(k, carry):
        query_copy(k).wait_recv()
        attend(k, ax_out.at[k])
        partial_copy(k).start()
        return carry

    lax.fori_loop(1, nc, serve, 0)

    wo_in.wait()
    a, b, c = three_parts(sv[...])
    line = iota((16, model), 0)
    folded = jnp.where(line == 0, a, jnp.where(line == 1, b, jnp.where(line == 2, c, 0.0)))
    w2[...] = jnp.sum(dot_last(folded.astype(BF16), wo[...]), axis=0, keepdims=True)
    own_docs = token_column(docs.astype(F32), p * toks)
    fin = fz.shape[2]
    member = (own_docs == iota((toks, fin), 1).astype(F32)).astype(F32)
    mine = p * doc_dev + iota((doc_dev, total_toks), 0)
    counts = jnp.sum((docs == mine).astype(F32), axis=1, keepdims=True)
    ow_in.wait()

    lanes = iota((128, width), 0)
    same = lanes % heads == iota((128, width), 1) // depth
    pick_top = (same & (lanes < 3 * heads)).astype(F32).astype(BF16)
    pick_total = (same & (lanes >= 3 * heads) & (lanes < 6 * heads)).astype(F32).astype(BF16)
    for k in range(1, nc):
        partial_copy(k).wait_recv()
    best = dot(ax[0, :, width:], pick_top)
    for k in range(1, nc):
        best = jnp.maximum(best, dot(ax[k, :, width:], pick_top))
    total = jnp.zeros((toks, width), F32)
    sums = jnp.zeros((toks, width), F32)
    for k in range(nc):
        stat = ax[k, :, width:]
        factor = jnp.exp(dot(stat, pick_top) - best)
        total += factor * dot(stat, pick_total)
        sums += factor * ax[k, :, :width].astype(F32)
    context = (sums / total).astype(BF16)

    def block_of(k):
        return pl.ds(pl.multiple_of(((z + k) % nz) * block, block), block)

    def scatter_copy(k):
        return pltpu.make_async_remote_copy(
            src_ref=rs_out.at[k], dst_ref=rs.at[k], send_sem=r_s.at[k], recv_sem=r_r.at[k],
            device_id=((z + k) % nz, p), device_id_type=MESH,
        )

    order = sorted(range(1, nz), key=lambda k: -min(k, nz - k))
    for k in order:
        rs_out[k] = dot(context, ow[:, block_of(k)]).astype(BF16)
        scatter_copy(k).start()
    hidden = doc[:, block_of(0)].astype(F32) + dot(context, ow[:, block_of(0)])
    for k in reversed(order):
        scatter_copy(k).wait_recv()
        hidden += rs[k].astype(F32)

    def gather_copy(k):
        return pltpu.make_async_remote_copy(
            src_ref=ag.at[0], dst_ref=ag.at[k], send_sem=g_s.at[k], recv_sem=g_r.at[k],
            device_id=((z + k) % nz, p), device_id_type=MESH,
        )

    gain = gf[:, block_of(0)]
    ag[0] = (hidden * gain).astype(BF16)
    for k in order:
        gather_copy(k).start()
    tok_score = jnp.sum(hidden * sv[:, block_of(0)], axis=1, keepdims=True)
    squares = jnp.sum(hidden * hidden, axis=1, keepdims=True)
    wg_in.wait()
    wu_in.wait()
    gate = dot(ag[0], wg[block_of(0), :])
    upper = dot(ag[0], wu[block_of(0), :])
    for k in reversed(order):
        gather_copy(k).wait_recv()
        rows = block_of(nz - k)
        piece = ag[k]
        gate += dot(piece, wg[rows, :])
        upper += dot(piece, wu[rows, :])
        plain = piece.astype(F32) / gf[:, rows]
        squares += jnp.sum(plain * plain, axis=1, keepdims=True)
    scale = lax.rsqrt(squares / model + 1e-6)
    gate = gate * scale
    upper = upper * scale
    middle = (jax.nn.gelu(gate, approximate=True) * upper).astype(BF16).astype(F32)
    tok_score += jnp.sum(middle * w2[...], axis=1, keepdims=True)

    fz[0] = jnp.broadcast_to(jnp.sum(member * tok_score, axis=0, keepdims=True), fz.shape[1:])

    def z_copy(k):
        return pltpu.make_async_remote_copy(
            src_ref=fz.at[0], dst_ref=fz.at[k], send_sem=z_s.at[k], recv_sem=z_r.at[k],
            device_id=((z + k) % nz, p), device_id_type=MESH,
        )

    def p_copy(k):
        return pltpu.make_async_remote_copy(
            src_ref=fp.at[0], dst_ref=fp.at[k], send_sem=p_s.at[k], recv_sem=p_r.at[k],
            device_id=(z, (p + k) % npg), device_id_type=MESH,
        )

    for k in order:
        z_copy(k).start()
    for k in order:
        z_copy(k).wait_recv()
    fp[0] = jnp.sum(fz[...], axis=0)
    for k in range(1, npg):
        p_copy(k).start()
    for k in range(1, npg):
        p_copy(k).wait_recv()
    pooled = jnp.sum(fp[...], axis=0)
    want = iota((doc_dev, fin), 1) == iota((doc_dev, fin), 0) + p * doc_dev
    picked = jnp.sum(jnp.where(want, pooled[0:1, :], 0.0), axis=1, keepdims=True)
    scores = picked / counts
    eye = iota((doc_dev, doc_dev), 0) == iota((doc_dev, doc_dev), 1)
    out[...] = jnp.sum(jnp.where(eye, scores, 0.0), axis=0, keepdims=True)

    for copy in pairs:
        copy.wait_send()
    for k in range(1, nc):
        query_copy(k).wait_send()
        partial_copy(k).wait_send()
    for k in range(1, nz):
        scatter_copy(k).wait_send()
        gather_copy(k).wait_send()
        z_copy(k).wait_send()
    for k in range(1, npg):
        p_copy(k).wait_send()


def per_device(
    nz, npg,
    doc_states, gain_attn, query_weight, cache_keys, cache_values, rel_bucket, bias_table,
    out_weight, gain_ffn, wi_gate, wi_up, wo_ffn, score_vector, query_lengths, doc_query,
    doc_of_token, page_table,
):
    toks, model = doc_states.shape
    width = query_weight.shape[1]
    hidden_units = wi_gate.shape[1]
    heads = bias_table.shape[1]
    pages, page_len, _ = cache_keys.shape
    total_toks = doc_of_token.shape[0]
    ndoc = doc_query.shape[0]
    nc = npg // 2
    span = 2 * pages * page_len
    block = model // nz
    fin = max(128, ndoc)
    hbm = pl.BlockSpec(memory_space=pl.ANY)
    vmem = pl.BlockSpec(memory_space=pltpu.VMEM)
    smem = pl.BlockSpec(memory_space=pltpu.SMEM)
    dma = pltpu.SemaphoreType.DMA
    result = pl.pallas_call(
        functools.partial(kernel, nz, npg),
        out_shape=jax.ShapeDtypeStruct((1, ndoc // npg), F32),
        in_specs=[
            hbm, vmem, hbm, hbm, hbm, vmem, vmem, hbm, vmem, hbm, hbm, hbm, vmem,
            smem, smem, vmem, smem,
        ],
        out_specs=vmem,
        scratch_shapes=[
            pltpu.VMEM((toks, model), BF16),
            pltpu.VMEM((model, width), BF16),
            pltpu.VMEM((2, pages, page_len, width), BF16),
            pltpu.VMEM((2, pages, page_len, width), BF16),
            pltpu.VMEM((pages, page_len), jnp.int32),
            pltpu.VMEM((width, model), BF16),
            pltpu.VMEM((model, hidden_units), BF16),
            pltpu.VMEM((model, hidden_units), BF16),
            pltpu.VMEM((hidden_units, model), BF16),
            pltpu.VMEM((heads, span, 128), BF16),
            pltpu.VMEM((heads, span, 128), BF16),
            pltpu.VMEM((heads, span), F32),
            pltpu.VMEM((1, total_toks), F32),
            pltpu.VMEM((1, span), F32),
            pltpu.VMEM((nc, toks, width), BF16),
            pltpu.VMEM((nc, toks, width + 128), BF16),
            pltpu.VMEM((nc, toks, width + 128), BF16),
            pltpu.VMEM((nz, toks, block), BF16),
            pltpu.VMEM((nz, toks, block), BF16),
            pltpu.VMEM((nz, toks, block), BF16),
            pltpu.VMEM((nz, 8, fin), F32),
            pltpu.VMEM((npg, 8, fin), F32),
            pltpu.VMEM((1, hidden_units), F32),
            dma((8,)), dma((3,)), dma((3,)),
            dma((nc,)), dma((nc,)), dma((nc,)), dma((nc,)),
            dma((nz,)), dma((nz,)), dma((nz,)), dma((nz,)), dma((nz,)), dma((nz,)),
            dma((npg,)), dma((npg,)),
        ],
        compiler_params=pltpu.CompilerParams(
            collective_id=0, has_side_effects=True, vmem_limit_bytes=48 * 2**20,
        ),
    )(
        doc_states, gain_attn.reshape(1, -1), query_weight, cache_keys, cache_values, rel_bucket,
        bias_table, out_weight, gain_ffn.reshape(1, -1), wi_gate, wi_up, wo_ffn,
        score_vector.reshape(1, -1), query_lengths, doc_query, doc_of_token.reshape(1, -1),
        page_table,
    )
    return result.reshape(-1)


def solution(mesh):
    return jax.shard_map(
        functools.partial(per_device, mesh.shape["head"], mesh.shape["page"]),
        mesh=mesh,
        in_specs=(
            P("page", None),
            P(),
            P(None, "head"),
            P("page", None, "head"),
            P("page", None, "head"),
            P("page", None),
            P(None, "head"),
            P("head", None),
            P(),
            P(None, "head"),
            P(None, "head"),
            P("head", None),
            P(),
            P(),
            P(),
            P(),
            P(),
        ),
        out_specs=P("page"),
        check_vma=False,
    )
```

```python
import functools

import jax
import jax.numpy as jnp
from jax import lax
from jax.experimental import pallas as pl
from jax.experimental.pallas import tpu as pltpu
from jax.sharding import PartitionSpec as P

NQ = 8
FAR = -1e30
MESH = pl.DeviceIdType.MESH
F32 = jnp.float32
BF16 = jnp.bfloat16


def iota(shape, dim):
    return lax.broadcasted_iota(jnp.int32, shape, dim)


def dot(a, b):
    return jnp.dot(a, b, preferred_element_type=F32)


def dot_last(a, b):
    return lax.dot_general(a, b, (((1,), (1,)), ((), ())), preferred_element_type=F32)


def three_parts(value):
    first = value.astype(BF16).astype(F32)
    second = (value - first).astype(BF16).astype(F32)
    third = (value - first - second).astype(BF16).astype(F32)
    return first, second, third


def kernel(
    nz, npg,
    doc_hbm, ga_hbm, qw_hbm, ck_hbm, cv_hbm, rb_hbm, bt_hbm, ow_hbm, gf_hbm, wg_hbm, wu_hbm,
    wo_hbm, sv_hbm, ql_hbm, dq_hbm, dtok_hbm, pt_hbm,
    out,
    ga, rb, bt, gf, sv, ql, dq, dtok, pt,
    doc, qw, kbuf, vbuf, rbx, ow, wg, wu, wo, kz, vz, kbias, tokq_row, keyq_row,
    q_all, ax_out, ax, rs_out, rs, ag, fz, fp, w2,
    lsem, pair_s, pair_r, q_s, q_r, a_s, a_r, r_s, r_r, g_s, g_r, z_s, z_r, p_s, p_r,
):
    nc = npg // 2
    z = lax.axis_index("head")
    p = lax.axis_index("page")
    core = p % 2
    chip = p // 2
    partner = p + 1 - 2 * core
    toks, model = doc.shape
    width = qw.shape[1]
    heads = bt.shape[0]
    depth = width // heads
    pages, page_len = rb.shape
    span = 2 * pages * page_len
    total_toks = dtok.shape[1]
    ndoc = dq.shape[0]
    doc_dev = ndoc // npg
    block = model // nz
    all_pages = pt.shape[0]
    max_pages = all_pages // NQ

    barrier = pltpu.get_barrier_semaphore()
    for k in range(1, npg):
        pl.semaphore_signal(barrier, inc=1, device_id=(z, (p + k) % npg), device_id_type=MESH)
    for k in range(1, nz):
        pl.semaphore_signal(barrier, inc=1, device_id=((z + k) % nz, p), device_id_type=MESH)

    moves = []
    for n, (src, dst) in enumerate([
        (doc_hbm, doc), (ga_hbm, ga), (qw_hbm, qw),
        (ck_hbm, kbuf.at[0]), (cv_hbm, vbuf.at[0]),
        (ow_hbm, ow), (wo_hbm, wo), (wg_hbm, wg), (wu_hbm, wu),
        (rb_hbm, rb), (bt_hbm, bt), (gf_hbm, gf), (sv_hbm, sv),
        (ql_hbm, ql), (dq_hbm, dq), (dtok_hbm, dtok), (pt_hbm, pt),
    ]):
        moves.append(pltpu.make_async_copy(src, dst, lsem.at[n]))
    doc_in, ga_in, qw_in, k_in, v_in, ow_in, wo_in, wg_in, wu_in = moves[:9]
    small_in = moves[9:]
    for move in [doc_in, ga_in, qw_in] + small_in + [k_in, v_in]:
        move.start()

    pl.semaphore_wait(barrier, npg - 1 + nz - 1)
    pairs = []
    for n, (src, dst) in enumerate([(ck_hbm, kbuf.at[1]), (cv_hbm, vbuf.at[1]), (rb_hbm, rbx)]):
        copy = pltpu.make_async_remote_copy(
            src_ref=src, dst_ref=dst, send_sem=pair_s.at[n], recv_sem=pair_r.at[n],
            device_id=(z, partner), device_id_type=MESH,
        )
        copy.start()
        pairs.append(copy)

    doc_in.wait()
    ga_in.wait()
    x = doc[...].astype(F32)
    scale = lax.rsqrt(jnp.mean(x * x, axis=1, keepdims=True) + 1e-6)
    normed = (x * scale * ga[...]).astype(BF16)
    qw_in.wait()
    q_all[0] = dot(normed, qw[...]).astype(BF16)

    def query_copy(k):
        return pltpu.make_async_remote_copy(
            src_ref=q_all.at[0], dst_ref=q_all.at[k], send_sem=q_s.at[k], recv_sem=q_r.at[k],
            device_id=(z, ((chip + k) % nc) * 2 + core), device_id_type=MESH,
        )

    for k in range(1, nc):
        query_copy(k).start()
    for move in (ow_in, wo_in, wg_in, wu_in):
        move.start()
    for move in small_in:
        move.wait()

    docs = dtok[...]

    def fill(step, carry):
        for j in range(16):
            d = step * 16 + j
            carry = jnp.where(docs == d, dq[d], carry)
        return carry

    tokq_row[...] = lax.fori_loop(
        0, ndoc // 16, fill, jnp.zeros((1, total_toks), jnp.int32)
    ).astype(F32)
    lane = iota((1, span), 1)
    half = span // 2
    page = jnp.where(lane < half, p * pages + lane // page_len, partner * pages + (lane - half) // page_len)
    owner = jnp.full((1, span), -1.0, F32)
    left = jnp.zeros((1, span), jnp.int32)
    for s in range(all_pages):
        hit = page == pt[s]
        owner = jnp.where(hit, float(s // max_pages), owner)
        left = jnp.where(hit, ql[s // max_pages] - (s % max_pages) * page_len, left)
    keyq_row[...] = jnp.where(lane % page_len < left, owner, -1.0)

    side = iota((1, 128), 1) // depth
    side_mask = [(side == s).astype(F32).astype(BF16) for s in range(128 // depth)]
    per = 128 // depth

    def split_heads(buf, dest, slot):
        for j in range(pages):
            rows = pl.ds((slot * pages + j) * page_len, page_len)
            for h in range(heads):
                g = h // per
                dest[h, rows, :] = buf[slot, j, :, g * 128:(g + 1) * 128] * side_mask[h % per]

    buckets = bt.shape[1]

    def bias_of(ref, slot):
        for j in range(pages):
            onehot = (ref[j:j + 1, :] == iota((buckets, page_len), 0)).astype(F32)
            part = lax.dot_general(
                bt[...], onehot, (((1,), (0,)), ((), ())),
                precision=lax.Precision.HIGHEST, preferred_element_type=F32,
            )
            at = (slot * pages + j) * page_len
            kbias[:, at:at + page_len] = part

    bias_of(rb, 0)
    k_in.wait()
    split_heads(kbuf, kz, 0)
    v_in.wait()
    split_heads(vbuf, vz, 0)
    for copy in pairs:
        copy.wait_recv()
    bias_of(rbx, 1)
    split_heads(kbuf, kz, 1)
    split_heads(vbuf, vz, 1)

    spot = iota((1, 128), 1)

    def token_column(row, first):
        hit = iota((toks, total_toks), 1) == iota((toks, total_toks), 0) + first
        return jnp.sum(jnp.where(hit, row, 0.0), axis=1, keepdims=True)

    def attend(k, dest):
        source = ((chip - k + nc) % nc) * 2 + core
        column = token_column(tokq_row[...], source * toks)
        far = jnp.where(column == keyq_row[...], 0.0, FAR)
        stats = jnp.zeros((toks, 128), F32)
        for base in range(0, heads, 4):
            some = range(base, base + 4)
            scores = [
                dot_last(q_all[k, :, h // per * 128:(h // per + 1) * 128], kz[h])
                + (far + kbias[h:h + 1, :])
                for h in some
            ]
            tops = [jnp.max(score, axis=1, keepdims=True) for score in scores]
            weights = [jnp.exp(score - top) for score, top in zip(scores, tops)]
            totals = [jnp.sum(weight, axis=1, keepdims=True) for weight in weights]
            parts = [dot(weight.astype(BF16), vz[h]) for weight, h in zip(weights, some)]
            for h, top, total in zip(some, tops, totals):
                mine = spot % heads == h
                stats = jnp.where(mine & (spot < 3 * heads), top, stats)
                stats = jnp.where(mine & (spot >= 3 * heads), total, stats)
            for j in range(0, 4, per):
                g = (base + j) // per
                dest[:, g * 128:(g + 1) * 128] = sum(parts[j:j + per]).astype(BF16)
        a, b, c = three_parts(stats)
        part = (spot // heads) % 3
        packed = jnp.where(part == 0, a, jnp.where(part == 1, b, c))
        dest[:, width:] = jnp.where(spot < 6 * heads, packed, 0.0).astype(BF16)

    def partial_copy(k):
        return pltpu.make_async_remote_copy(
            src_ref=ax_out.at[k], dst_ref=ax.at[k], send_sem=a_s.at[k], recv_sem=a_r.at[k],
            device_id=(z, ((chip - k + nc) % nc) * 2 + core), device_id_type=MESH,
        )

    attend(0, ax.at[0])

    def serve(k, carry):
        query_copy(k).wait_recv()
        attend(k, ax_out.at[k])
        partial_copy(k).start()
        return carry

    lax.fori_loop(1, nc, serve, 0)

    wo_in.wait()
    a, b, c = three_parts(sv[...])
    line = iota((16, model), 0)
    folded = jnp.where(line == 0, a, jnp.where(line == 1, b, jnp.where(line == 2, c, 0.0)))
    w2[...] = jnp.sum(dot_last(folded.astype(BF16), wo[...]), axis=0, keepdims=True)
    own_docs = token_column(docs.astype(F32), p * toks)
    fin = fz.shape[2]
    member = (own_docs == iota((toks, fin), 1).astype(F32)).astype(F32)
    mine = p * doc_dev + iota((doc_dev, total_toks), 0)
    counts = jnp.sum((docs == mine).astype(F32), axis=1, keepdims=True)
    ow_in.wait()

    lanes = iota((128, width), 0)
    same = lanes % heads == iota((128, width), 1) // depth
    pick_top = (same & (lanes < 3 * heads)).astype(F32).astype(BF16)
    pick_total = (same & (lanes >= 3 * heads) & (lanes < 6 * heads)).astype(F32).astype(BF16)
    for k in range(1, nc):
        partial_copy(k).wait_recv()
    best = dot(ax[0, :, width:], pick_top)
    for k in range(1, nc):
        best = jnp.maximum(best, dot(ax[k, :, width:], pick_top))
    total = jnp.zeros((toks, width), F32)
    sums = jnp.zeros((toks, width), F32)
    for k in range(nc):
        stat = ax[k, :, width:]
        factor = jnp.exp(dot(stat, pick_top) - best)
        total += factor * dot(stat, pick_total)
        sums += factor * ax[k, :, :width].astype(F32)
    context = (sums / total).astype(BF16)

    def block_of(k):
        return pl.ds(pl.multiple_of(((z + k) % nz) * block, block), block)

    def scatter_copy(k):
        return pltpu.make_async_remote_copy(
            src_ref=rs_out.at[k], dst_ref=rs.at[k], send_sem=r_s.at[k], recv_sem=r_r.at[k],
            device_id=((z + k) % nz, p), device_id_type=MESH,
        )

    order = sorted(range(1, nz), key=lambda k: -min(k, nz - k))
    for k in order:
        rs_out[k] = dot(context, ow[:, block_of(k)]).astype(BF16)
        scatter_copy(k).start()
    hidden = doc[:, block_of(0)].astype(F32) + dot(context, ow[:, block_of(0)])
    for k in reversed(order):
        scatter_copy(k).wait_recv()
        hidden += rs[k].astype(F32)

    def gather_copy(k):
        return pltpu.make_async_remote_copy(
            src_ref=ag.at[0], dst_ref=ag.at[k], send_sem=g_s.at[k], recv_sem=g_r.at[k],
            device_id=((z + k) % nz, p), device_id_type=MESH,
        )

    gain = gf[:, block_of(0)]
    ag[0] = (hidden * gain).astype(BF16)
    for k in order:
        gather_copy(k).start()
    tok_score = jnp.sum(hidden * sv[:, block_of(0)], axis=1, keepdims=True)
    squares = jnp.sum(hidden * hidden, axis=1, keepdims=True)
    wg_in.wait()
    wu_in.wait()
    gate = dot(ag[0], wg[block_of(0), :])
    upper = dot(ag[0], wu[block_of(0), :])
    for k in reversed(order):
        gather_copy(k).wait_recv()
        rows = block_of(nz - k)
        piece = ag[k]
        gate += dot(piece, wg[rows, :])
        upper += dot(piece, wu[rows, :])
        plain = piece.astype(F32) / gf[:, rows]
        squares += jnp.sum(plain * plain, axis=1, keepdims=True)
    scale = lax.rsqrt(squares / model + 1e-6)
    gate = gate * scale
    upper = upper * scale
    middle = (jax.nn.gelu(gate, approximate=True) * upper).astype(BF16).astype(F32)
    tok_score += jnp.sum(middle * w2[...], axis=1, keepdims=True)

    fz[0] = jnp.broadcast_to(jnp.sum(member * tok_score, axis=0, keepdims=True), fz.shape[1:])

    def z_copy(k):
        return pltpu.make_async_remote_copy(
            src_ref=fz.at[0], dst_ref=fz.at[k], send_sem=z_s.at[k], recv_sem=z_r.at[k],
            device_id=((z + k) % nz, p), device_id_type=MESH,
        )

    def p_copy(k):
        return pltpu.make_async_remote_copy(
            src_ref=fp.at[0], dst_ref=fp.at[k], send_sem=p_s.at[k], recv_sem=p_r.at[k],
            device_id=(z, (p + k) % npg), device_id_type=MESH,
        )

    for k in order:
        z_copy(k).start()
    for k in order:
        z_copy(k).wait_recv()
    fp[0] = jnp.sum(fz[...], axis=0)
    for k in range(1, npg):
        p_copy(k).start()
    for k in range(1, npg):
        p_copy(k).wait_recv()
    pooled = jnp.sum(fp[...], axis=0)
    want = iota((doc_dev, fin), 1) == iota((doc_dev, fin), 0) + p * doc_dev
    picked = jnp.sum(jnp.where(want, pooled[0:1, :], 0.0), axis=1, keepdims=True)
    scores = picked / counts
    eye = iota((doc_dev, doc_dev), 0) == iota((doc_dev, doc_dev), 1)
    out[...] = jnp.sum(jnp.where(eye, scores, 0.0), axis=0, keepdims=True)

    for copy in pairs:
        copy.wait_send()
    for k in range(1, nc):
        query_copy(k).wait_send()
        partial_copy(k).wait_send()
    for k in range(1, nz):
        scatter_copy(k).wait_send()
        gather_copy(k).wait_send()
        z_copy(k).wait_send()
    for k in range(1, npg):
        p_copy(k).wait_send()


def per_device(
    nz, npg,
    doc_states, gain_attn, query_weight, cache_keys, cache_values, rel_bucket, bias_table,
    out_weight, gain_ffn, wi_gate, wi_up, wo_ffn, score_vector, query_lengths, doc_query,
    doc_of_token, page_table,
):
    toks, model = doc_states.shape
    width = query_weight.shape[1]
    hidden_units = wi_gate.shape[1]
    heads, buckets = bias_table.shape[1], bias_table.shape[0]
    pages, page_len, _ = cache_keys.shape
    total_toks = doc_of_token.shape[0]
    ndoc = doc_query.shape[0]
    nc = npg // 2
    span = 2 * pages * page_len
    block = model // nz
    fin = max(128, ndoc)
    hbm = pl.BlockSpec(memory_space=pltpu.HBM)
    vmem = pl.BlockSpec(memory_space=pltpu.VMEM)
    dma = pltpu.SemaphoreType.DMA
    result = pl.pallas_call(
        functools.partial(kernel, nz, npg),
        out_shape=jax.ShapeDtypeStruct((1, ndoc // npg), F32),
        in_specs=[hbm] * 17,
        out_specs=vmem,
        scratch_shapes=[
            pltpu.VMEM((1, model), F32),
            pltpu.VMEM((pages, page_len), jnp.int32),
            pltpu.VMEM((heads, buckets), F32),
            pltpu.VMEM((1, model), F32),
            pltpu.VMEM((1, model), F32),
            pltpu.SMEM(query_lengths.shape, jnp.int32),
            pltpu.SMEM(doc_query.shape, jnp.int32),
            pltpu.VMEM((1, total_toks), jnp.int32),
            pltpu.SMEM(page_table.shape, jnp.int32),
            pltpu.VMEM((toks, model), BF16),
            pltpu.VMEM((model, width), BF16),
            pltpu.VMEM((2, pages, page_len, width), BF16),
            pltpu.VMEM((2, pages, page_len, width), BF16),
            pltpu.VMEM((pages, page_len), jnp.int32),
            pltpu.VMEM((width, model), BF16),
            pltpu.VMEM((model, hidden_units), BF16),
            pltpu.VMEM((model, hidden_units), BF16),
            pltpu.VMEM((hidden_units, model), BF16),
            pltpu.VMEM((heads, span, 128), BF16),
            pltpu.VMEM((heads, span, 128), BF16),
            pltpu.VMEM((heads, span), F32),
            pltpu.VMEM((1, total_toks), F32),
            pltpu.VMEM((1, span), F32),
            pltpu.VMEM((nc, toks, width), BF16),
            pltpu.VMEM((nc, toks, width + 128), BF16),
            pltpu.VMEM((nc, toks, width + 128), BF16),
            pltpu.VMEM((nz, toks, block), BF16),
            pltpu.VMEM((nz, toks, block), BF16),
            pltpu.VMEM((nz, toks, block), BF16),
            pltpu.VMEM((nz, 8, fin), F32),
            pltpu.VMEM((npg, 8, fin), F32),
            pltpu.VMEM((1, hidden_units), F32),
            dma((17,)), dma((3,)), dma((3,)),
            dma((nc,)), dma((nc,)), dma((nc,)), dma((nc,)),
            dma((nz,)), dma((nz,)), dma((nz,)), dma((nz,)), dma((nz,)), dma((nz,)),
            dma((npg,)), dma((npg,)),
        ],
        compiler_params=pltpu.CompilerParams(
            collective_id=0, has_side_effects=True, vmem_limit_bytes=56 * 2**20,
        ),
    )(
        doc_states, gain_attn.reshape(1, -1), query_weight, cache_keys, cache_values, rel_bucket,
        bias_table.T, out_weight, gain_ffn.reshape(1, -1), wi_gate, wi_up, wo_ffn,
        score_vector.reshape(1, -1), query_lengths, doc_query, doc_of_token.reshape(1, -1),
        page_table,
    )
    return result.reshape(-1)


def solution(mesh):
    return jax.shard_map(
        functools.partial(per_device, mesh.shape["head"], mesh.shape["page"]),
        mesh=mesh,
        in_specs=(
            P("page", None),
            P(),
            P(None, "head"),
            P("page", None, "head"),
            P("page", None, "head"),
            P("page", None),
            P(None, "head"),
            P("head", None),
            P(),
            P(None, "head"),
            P(None, "head"),
            P("head", None),
            P(),
            P(),
            P(),
            P(),
            P(),
        ),
        out_specs=P("page"),
        check_vma=False,
    )
```

```python
import functools

import jax
import jax.numpy as jnp
from jax import lax
from jax.experimental import pallas as pl
from jax.experimental.pallas import tpu as pltpu
from jax.sharding import PartitionSpec as P

NQ = 8
FAR = -1e30
MESH = pl.DeviceIdType.MESH
F32 = jnp.float32
BF16 = jnp.bfloat16


def iota(shape, dim):
    return lax.broadcasted_iota(jnp.int32, shape, dim)


def dot(a, b):
    return jnp.dot(a, b, preferred_element_type=F32)


def three_parts(value):
    first = value.astype(BF16).astype(F32)
    second = (value - first).astype(BF16).astype(F32)
    third = (value - first - second).astype(BF16).astype(F32)
    return first, second, third


def kernel(
    nz, npg,
    doc_hbm, ga_hbm, qw_hbm, ck_hbm, cv_hbm, rb_hbm, bt_hbm, ow_hbm, gf_hbm, wg_hbm, wu_hbm,
    wo_hbm, sv_hbm, ql_hbm, dq_hbm, dtok_hbm, pt_hbm,
    out,
    ga, rb, bt, gf, sv, ql, dq, dtok, pt,
    doc, qw, kbuf, vbuf, rbx, ow, wg, wu, wo, kz, vz, kbias, tokq_row, keyq_row,
    q_all, ax_out, ax, rs_out, rs, ag, fz, fp, svt, w2,
    lsem, pair_s, pair_r, q_s, q_r, a_s, a_r, r_s, r_r, g_s, g_r, z_s, z_r, p_s, p_r,
):
    nc = npg // 2
    group = 3 if (nc - 1) % 3 == 0 else 1
    z = lax.axis_index("head")
    p = lax.axis_index("page")
    core = p % 2
    chip = p // 2
    partner = p + 1 - 2 * core
    toks, model = doc.shape
    width = qw.shape[1]
    heads = bt.shape[0]
    depth = width // heads
    pages, page_len = rb.shape
    span = 2 * pages * page_len
    total_toks = dtok.shape[1]
    ndoc = dq.shape[0]
    doc_dev = ndoc // npg
    block = model // nz
    part = toks // 2
    all_pages = pt.shape[0]
    max_pages = all_pages // NQ

    barrier = pltpu.get_barrier_semaphore()
    for k in range(1, npg):
        pl.semaphore_signal(barrier, inc=1, device_id=(z, (p + k) % npg), device_id_type=MESH)
    for k in range(1, nz):
        pl.semaphore_signal(barrier, inc=1, device_id=((z + k) % nz, p), device_id_type=MESH)

    moves = []
    for n, (src, dst) in enumerate([
        (doc_hbm, doc), (ga_hbm, ga), (qw_hbm, qw),
        (ck_hbm, kbuf.at[0]), (cv_hbm, vbuf.at[0]),
        (ow_hbm, ow), (wo_hbm, wo), (wg_hbm, wg), (wu_hbm, wu),
        (rb_hbm, rb), (bt_hbm, bt), (gf_hbm, gf), (sv_hbm, sv),
        (ql_hbm, ql), (dq_hbm, dq), (dtok_hbm, dtok), (pt_hbm, pt),
    ]):
        moves.append(pltpu.make_async_copy(src, dst, lsem.at[n]))
    doc_in, ga_in, qw_in, k_in, v_in, ow_in, wo_in, wg_in, wu_in = moves[:9]
    small_in = moves[9:]
    for move in [doc_in, ga_in, qw_in] + small_in + [k_in, v_in]:
        move.start()

    pl.semaphore_wait(barrier, npg - 1 + nz - 1)
    pairs = []
    for n, (src, dst) in enumerate([(ck_hbm, kbuf.at[1]), (cv_hbm, vbuf.at[1]), (rb_hbm, rbx)]):
        copy = pltpu.make_async_remote_copy(
            src_ref=src, dst_ref=dst, send_sem=pair_s.at[n], recv_sem=pair_r.at[n],
            device_id=(z, partner), device_id_type=MESH,
        )
        copy.start()
        pairs.append(copy)

    doc_in.wait()
    ga_in.wait()
    x = doc[...].astype(F32)
    scale = lax.rsqrt(jnp.mean(x * x, axis=1, keepdims=True) + 1e-6)
    normed = (x * scale * ga[...]).astype(BF16)
    qw_in.wait()
    q_all[0] = dot(normed, qw[...]).astype(BF16)

    def rows_of(a):
        return pl.ds(a * part, part)

    def query_copy(k, a):
        return pltpu.make_async_remote_copy(
            src_ref=q_all.at[0, rows_of(a)], dst_ref=q_all.at[k, rows_of(a)],
            send_sem=q_s.at[a, k], recv_sem=q_r.at[a, k],
            device_id=(z, ((chip + k) % nc) * 2 + core), device_id_type=MESH,
        )

    for a in range(2):
        for k in range(1, nc):
            query_copy(k, a).start()
    for move in (ow_in, wo_in, wg_in, wu_in):
        move.start()
    for move in small_in:
        move.wait()

    docs = dtok[...]

    def fill(step, carry):
        for j in range(16):
            d = step * 16 + j
            carry = jnp.where(docs == d, dq[d], carry)
        return carry

    tokq_row[...] = lax.fori_loop(
        0, ndoc // 16, fill, jnp.zeros((1, total_toks), jnp.int32)
    ).astype(F32)
    lane = iota((1, span), 1)
    half = span // 2
    page = jnp.where(lane < half, p * pages + lane // page_len, partner * pages + (lane - half) // page_len)
    owner = jnp.full((1, span), -1.0, F32)
    left = jnp.zeros((1, span), jnp.int32)
    for s in range(all_pages):
        hit = page == pt[s]
        owner = jnp.where(hit, float(s // max_pages), owner)
        left = jnp.where(hit, ql[s // max_pages] - (s % max_pages) * page_len, left)
    keyq_row[...] = jnp.where(lane % page_len < left, owner, -1.0)

    side = iota((1, 128), 1) // depth
    side_mask = [(side == s).astype(F32).astype(BF16) for s in range(128 // depth)]
    per = 128 // depth

    tall = iota((128, 1), 0) // depth
    tall_mask = [(tall == s).astype(F32) for s in range(per)]

    def split_keys(slot):
        for j in range(pages):
            first = (slot * pages + j) * page_len
            for g in range(width // 128):
                flipped = kbuf[slot, j, :, g * 128:(g + 1) * 128].astype(F32).T
                for s in range(per):
                    kz[g * per + s, :, first:first + page_len] = (flipped * tall_mask[s]).astype(BF16)

    def split_values(slot):
        for j in range(pages):
            first = (slot * pages + j) * page_len
            for h in range(heads):
                g = h // per
                vz[h, first:first + page_len, :] = (
                    vbuf[slot, j, :, g * 128:(g + 1) * 128] * side_mask[h % per]
                )

    buckets = bt.shape[1]

    def bias_of(ref, slot):
        for j in range(pages):
            onehot = (ref[j:j + 1, :] == iota((buckets, page_len), 0)).astype(F32)
            part = lax.dot_general(
                bt[...], onehot, (((1,), (0,)), ((), ())),
                precision=lax.Precision.HIGHEST, preferred_element_type=F32,
            )
            at = (slot * pages + j) * page_len
            kbias[:, at:at + page_len] = part

    bias_of(rb, 0)
    k_in.wait()
    split_keys(0)
    v_in.wait()
    split_values(0)
    for copy in pairs:
        copy.wait_recv()
    bias_of(rbx, 1)
    split_keys(1)
    split_values(1)

    spot = iota((1, 128), 1)

    def token_column(row, first, count):
        hit = iota((count, total_toks), 1) == iota((count, total_toks), 0) + first
        return jnp.sum(jnp.where(hit, row, 0.0), axis=1, keepdims=True)

    def attend(load, column):
        far = jnp.where(column == keyq_row[...], 0.0, FAR)
        stats = jnp.zeros((column.shape[0], 128), F32)
        pieces = []
        for base in range(0, heads, 4):
            some = range(base, base + 4)
            scores = [dot(load(h // per), kz[h]) + (far + kbias[h:h + 1, :]) for h in some]
            tops = [jnp.max(score, axis=1, keepdims=True) for score in scores]
            weights = [jnp.exp(score - top) for score, top in zip(scores, tops)]
            totals = [jnp.sum(weight, axis=1, keepdims=True) for weight in weights]
            parts = [dot(weight.astype(BF16), vz[h]) for weight, h in zip(weights, some)]
            for h, top, total in zip(some, tops, totals):
                own = spot % heads == h
                stats = jnp.where(own & (spot < 3 * heads), top, stats)
                stats = jnp.where(own & (spot >= 3 * heads), total, stats)
            for j in range(0, 4, per):
                pieces.append(sum(parts[j:j + per]).astype(BF16))
        first, second, third = three_parts(stats)
        turn = (spot // heads) % 3
        packed = jnp.where(turn == 0, first, jnp.where(turn == 1, second, third))
        pieces.append(jnp.where(spot < 6 * heads, packed, 0.0).astype(BF16))
        return pieces

    def partial_copy(k, a):
        return pltpu.make_async_remote_copy(
            src_ref=ax_out.at[k, rows_of(a)], dst_ref=ax.at[k, rows_of(a)],
            send_sem=a_s.at[a, k], recv_sem=a_r.at[a, k],
            device_id=(z, ((chip - k + nc) % nc) * 2 + core), device_id_type=MESH,
        )

    own = attend(
        lambda g: q_all[0, :, g * 128:(g + 1) * 128], token_column(tokq_row[...], p * toks, toks)
    )
    for g, piece in enumerate(own):
        ax[0, :, g * 128:(g + 1) * 128] = piece

    def serve(a, first):
        ks = [first + n for n in range(group)]
        for k in ks:
            query_copy(k, a).wait_recv()
        column = jnp.concatenate([
            token_column(
                tokq_row[...], (((chip - k + nc) % nc) * 2 + core) * toks + a * part, part
            )
            for k in ks
        ], axis=0)

        def load(g):
            return jnp.concatenate(
                [q_all[k, a * part:(a + 1) * part, g * 128:(g + 1) * 128] for k in ks], axis=0
            )

        for g, piece in enumerate(attend(load, column)):
            for n, k in enumerate(ks):
                ax_out[k, a * part:(a + 1) * part, g * 128:(g + 1) * 128] = (
                    piece[n * part:(n + 1) * part]
                )
        for k in ks:
            partial_copy(k, a).start()

    for a in range(2):
        if group == nc - 1:
            serve(a, 1)
        else:
            def step(n, carry):
                serve(a, 1 + n * group)
                return carry

            lax.fori_loop(0, (nc - 1) // group, step, 0)

    lanes = iota((128, width), 0)
    same = lanes % heads == iota((128, width), 1) // depth
    pick_top = (same & (lanes < 3 * heads)).astype(F32).astype(BF16)
    pick_total = (same & (lanes >= 3 * heads) & (lanes < 6 * heads)).astype(F32).astype(BF16)

    def join(a):
        rows = slice(a * part, (a + 1) * part)
        for k in range(1, nc):
            partial_copy(k, a).wait_recv()
        tops = [dot(ax[k, rows, width:], pick_top) for k in range(nc)]
        best = functools.reduce(jnp.maximum, tops)
        total = jnp.zeros((part, width), F32)
        sums = jnp.zeros((part, width), F32)
        for k in range(nc):
            factor = jnp.exp(tops[k] - best)
            total += factor * dot(ax[k, rows, width:], pick_total)
            sums += factor * ax[k, rows, :width].astype(F32)
        return (sums / total).astype(BF16)

    def block_of(k):
        return pl.ds(pl.multiple_of(((z + k) % nz) * block, block), block)

    def scatter_copy(k, a):
        return pltpu.make_async_remote_copy(
            src_ref=rs_out.at[k, rows_of(a)], dst_ref=rs.at[k, rows_of(a)],
            send_sem=r_s.at[a, k], recv_sem=r_r.at[a, k],
            device_id=((z + k) % nz, p), device_id_type=MESH,
        )

    def gather_copy(k, a):
        return pltpu.make_async_remote_copy(
            src_ref=ag.at[0, rows_of(a)], dst_ref=ag.at[k, rows_of(a)],
            send_sem=g_s.at[a, k], recv_sem=g_r.at[a, k],
            device_id=((z + k) % nz, p), device_id_type=MESH,
        )

    order = sorted(range(1, nz), key=lambda k: -min(k, nz - k))
    ow_in.wait()
    halves = []
    for a in range(2):
        rows = slice(a * part, (a + 1) * part)
        context = join(a)
        for k in order:
            rs_out[k, rows, :] = dot(context, ow[:, block_of(k)]).astype(BF16)
            scatter_copy(k, a).start()
        halves.append(doc[rows, block_of(0)].astype(F32) + dot(context, ow[:, block_of(0)]))

    wo_in.wait()
    first, second, third = three_parts(sv[...])
    line = iota((128, model), 0)
    folded = jnp.where(line == 0, first, jnp.where(line == 1, second, jnp.where(line == 2, third, 0.0)))
    for n in range(model // 128):
        svt[n * 128:(n + 1) * 128, :] = folded[:, n * 128:(n + 1) * 128].T.astype(BF16)
    tall_w = jnp.sum(dot(wo[...], svt[...]), axis=1, keepdims=True)
    first, second, third = three_parts(tall_w)
    w2[...] = jnp.where(
        spot == 0, first, jnp.where(spot == 1, second, jnp.where(spot == 2, third, 0.0))
    ).astype(BF16)
    own_docs = token_column(docs.astype(F32), p * toks, toks)
    fin = fz.shape[2]
    member = (own_docs == iota((toks, fin), 1).astype(F32)).astype(F32)
    mine = p * doc_dev + iota((doc_dev, total_toks), 0)
    counts = jnp.sum((docs == mine).astype(F32), axis=1, keepdims=True)

    gain = gf[:, block_of(0)]
    for a in range(2):
        rows = slice(a * part, (a + 1) * part)
        for k in reversed(order):
            scatter_copy(k, a).wait_recv()
            halves[a] += rs[k, rows, :].astype(F32)
        ag[0, rows, :] = (halves[a] * gain).astype(BF16)
        for k in order:
            gather_copy(k, a).start()
    hidden = jnp.concatenate(halves, axis=0)
    tok_score = jnp.sum(hidden * sv[:, block_of(0)], axis=1, keepdims=True)
    squares = jnp.sum(hidden * hidden, axis=1, keepdims=True)
    wg_in.wait()
    wu_in.wait()
    gate = dot(ag[0], wg[block_of(0), :])
    upper = dot(ag[0], wu[block_of(0), :])
    for k in reversed(order):
        gather_copy(k, 0).wait_recv()
        gather_copy(k, 1).wait_recv()
        rows = block_of(nz - k)
        piece = ag[k]
        gate += dot(piece, wg[rows, :])
        upper += dot(piece, wu[rows, :])
        plain = piece.astype(F32) / gf[:, rows]
        squares += jnp.sum(plain * plain, axis=1, keepdims=True)
    scale = lax.rsqrt(squares / model + 1e-6)
    gate = gate * scale
    upper = upper * scale
    middle = (jax.nn.gelu(gate, approximate=True) * upper).astype(BF16)
    tok_score += jnp.sum(dot(middle, w2[...]), axis=1, keepdims=True)

    fz[0] = jnp.broadcast_to(jnp.sum(member * tok_score, axis=0, keepdims=True), fz.shape[1:])

    def z_copy(k):
        return pltpu.make_async_remote_copy(
            src_ref=fz.at[0], dst_ref=fz.at[k], send_sem=z_s.at[k], recv_sem=z_r.at[k],
            device_id=((z + k) % nz, p), device_id_type=MESH,
        )

    def p_copy(k):
        return pltpu.make_async_remote_copy(
            src_ref=fp.at[0], dst_ref=fp.at[k], send_sem=p_s.at[k], recv_sem=p_r.at[k],
            device_id=(z, (p + k) % npg), device_id_type=MESH,
        )

    for k in order:
        z_copy(k).start()
    for k in order:
        z_copy(k).wait_recv()
    fp[0] = jnp.sum(fz[...], axis=0)
    for k in range(1, npg):
        p_copy(k).start()
    for k in range(1, npg):
        p_copy(k).wait_recv()
    pooled = jnp.sum(fp[...], axis=0)
    want = iota((doc_dev, fin), 1) == iota((doc_dev, fin), 0) + p * doc_dev
    picked = jnp.sum(jnp.where(want, pooled[0:1, :], 0.0), axis=1, keepdims=True)
    scores = picked / counts
    eye = iota((doc_dev, doc_dev), 0) == iota((doc_dev, doc_dev), 1)
    out[...] = jnp.sum(jnp.where(eye, scores, 0.0), axis=0, keepdims=True)

    for copy in pairs:
        copy.wait_send()
    for a in range(2):
        for k in range(1, nc):
            query_copy(k, a).wait_send()
            partial_copy(k, a).wait_send()
        for k in range(1, nz):
            scatter_copy(k, a).wait_send()
            gather_copy(k, a).wait_send()
    for k in range(1, nz):
        z_copy(k).wait_send()
    for k in range(1, npg):
        p_copy(k).wait_send()


def per_device(
    nz, npg,
    doc_states, gain_attn, query_weight, cache_keys, cache_values, rel_bucket, bias_table,
    out_weight, gain_ffn, wi_gate, wi_up, wo_ffn, score_vector, query_lengths, doc_query,
    doc_of_token, page_table,
):
    toks, model = doc_states.shape
    width = query_weight.shape[1]
    hidden_units = wi_gate.shape[1]
    heads, buckets = bias_table.shape[1], bias_table.shape[0]
    pages, page_len, _ = cache_keys.shape
    total_toks = doc_of_token.shape[0]
    ndoc = doc_query.shape[0]
    nc = npg // 2
    span = 2 * pages * page_len
    block = model // nz
    fin = max(128, ndoc)
    hbm = pl.BlockSpec(memory_space=pltpu.HBM)
    vmem = pl.BlockSpec(memory_space=pltpu.VMEM)
    dma = pltpu.SemaphoreType.DMA
    result = pl.pallas_call(
        functools.partial(kernel, nz, npg),
        out_shape=jax.ShapeDtypeStruct((1, ndoc // npg), F32),
        in_specs=[hbm] * 17,
        out_specs=vmem,
        scratch_shapes=[
            pltpu.VMEM((1, model), F32),
            pltpu.VMEM((pages, page_len), jnp.int32),
            pltpu.VMEM((heads, buckets), F32),
            pltpu.VMEM((1, model), F32),
            pltpu.VMEM((1, model), F32),
            pltpu.SMEM(query_lengths.shape, jnp.int32),
            pltpu.SMEM(doc_query.shape, jnp.int32),
            pltpu.VMEM((1, total_toks), jnp.int32),
            pltpu.SMEM(page_table.shape, jnp.int32),
            pltpu.VMEM((toks, model), BF16),
            pltpu.VMEM((model, width), BF16),
            pltpu.VMEM((2, pages, page_len, width), BF16),
            pltpu.VMEM((2, pages, page_len, width), BF16),
            pltpu.VMEM((pages, page_len), jnp.int32),
            pltpu.VMEM((width, model), BF16),
            pltpu.VMEM((model, hidden_units), BF16),
            pltpu.VMEM((model, hidden_units), BF16),
            pltpu.VMEM((hidden_units, model), BF16),
            pltpu.VMEM((heads, 128, span), BF16),
            pltpu.VMEM((heads, span, 128), BF16),
            pltpu.VMEM((heads, span), F32),
            pltpu.VMEM((1, total_toks), F32),
            pltpu.VMEM((1, span), F32),
            pltpu.VMEM((nc, toks, width), BF16),
            pltpu.VMEM((nc, toks, width + 128), BF16),
            pltpu.VMEM((nc, toks, width + 128), BF16),
            pltpu.VMEM((nz, toks, block), BF16),
            pltpu.VMEM((nz, toks, block), BF16),
            pltpu.VMEM((nz, toks, block), BF16),
            pltpu.VMEM((nz, 8, fin), F32),
            pltpu.VMEM((npg, 8, fin), F32),
            pltpu.VMEM((model, 128), BF16),
            pltpu.VMEM((hidden_units, 128), BF16),
            dma((17,)), dma((3,)), dma((3,)),
            dma((2, nc)), dma((2, nc)), dma((2, nc)), dma((2, nc)),
            dma((2, nz)), dma((2, nz)), dma((2, nz)), dma((2, nz)), dma((nz,)), dma((nz,)),
            dma((npg,)), dma((npg,)),
        ],
        compiler_params=pltpu.CompilerParams(
            collective_id=0, has_side_effects=True, vmem_limit_bytes=56 * 2**20,
        ),
    )(
        doc_states, gain_attn.reshape(1, -1), query_weight, cache_keys, cache_values, rel_bucket,
        bias_table.T, out_weight, gain_ffn.reshape(1, -1), wi_gate, wi_up, wo_ffn,
        score_vector.reshape(1, -1), query_lengths, doc_query, doc_of_token.reshape(1, -1),
        page_table,
    )
    return result.reshape(-1)


def solution(mesh):
    return jax.shard_map(
        functools.partial(per_device, mesh.shape["head"], mesh.shape["page"]),
        mesh=mesh,
        in_specs=(
            P("page", None),
            P(),
            P(None, "head"),
            P("page", None, "head"),
            P("page", None, "head"),
            P("page", None),
            P(None, "head"),
            P("head", None),
            P(),
            P(None, "head"),
            P(None, "head"),
            P("head", None),
            P(),
            P(),
            P(),
            P(),
            P(),
        ),
        out_specs=P("page"),
        check_vma=False,
    )
```

```python
import functools

import jax
import jax.numpy as jnp
from jax import lax
from jax.experimental import pallas as pl
from jax.experimental.pallas import tpu as pltpu
from jax.sharding import PartitionSpec as P

NQ = 8
FAR = -1e30
MESH = pl.DeviceIdType.MESH
F32 = jnp.float32
BF16 = jnp.bfloat16


def iota(shape, dim):
    return lax.broadcasted_iota(jnp.int32, shape, dim)


def dot(a, b):
    return jnp.dot(a, b, preferred_element_type=F32)


def three_parts(value):
    first = value.astype(BF16).astype(F32)
    second = (value - first).astype(BF16).astype(F32)
    third = (value - first - second).astype(BF16).astype(F32)
    return first, second, third


def kernel(
    nz, npg,
    doc_hbm, ga_hbm, qw_hbm, ck_hbm, cv_hbm, rb_hbm, bt_hbm, ow_hbm, gf_hbm, wg_hbm, wu_hbm,
    wo_hbm, sv_hbm, ql_hbm, dq_hbm, dtok_hbm, pt_hbm,
    out,
    ga, rb, bt, gf, sv, ql, dq, dtok, pt,
    doc, qw, kbuf, vbuf, rbx, ow, wg, wu, wo, kz, vz, kbias, tokq_row, keyq_row,
    q_all, ax_out, ax, rs_out, rs, ag, fz, fp, svt, w2,
    lsem, pair_s, pair_r, q_s, q_r, a_s, a_r, r_s, r_r, g_s, g_r, z_s, z_r, p_s, p_r,
):
    nc = npg // 2
    group = 3 if (nc - 1) % 3 == 0 else 1
    z = lax.axis_index("head")
    p = lax.axis_index("page")
    core = p % 2
    chip = p // 2
    partner = p + 1 - 2 * core
    toks, model = doc.shape
    width = qw.shape[1]
    heads = bt.shape[0]
    depth = width // heads
    pages, page_len = rb.shape
    span = 2 * pages * page_len
    total_toks = dtok.shape[1]
    ndoc = dq.shape[0]
    doc_dev = ndoc // npg
    block = model // nz
    part = toks // 2
    all_pages = pt.shape[0]
    max_pages = all_pages // NQ

    barrier = pltpu.get_barrier_semaphore()
    for k in range(1, npg):
        pl.semaphore_signal(barrier, inc=1, device_id=(z, (p + k) % npg), device_id_type=MESH)
    for k in range(1, nz):
        pl.semaphore_signal(barrier, inc=1, device_id=((z + k) % nz, p), device_id_type=MESH)

    moves = []
    for n, (src, dst) in enumerate([
        (doc_hbm, doc), (ga_hbm, ga),
        (ck_hbm, kbuf.at[0]), (cv_hbm, vbuf.at[0]),
        (ow_hbm, ow), (wo_hbm, wo), (wg_hbm, wg), (wu_hbm, wu),
        (rb_hbm, rb), (bt_hbm, bt), (gf_hbm, gf), (sv_hbm, sv),
        (ql_hbm, ql), (dq_hbm, dq), (dtok_hbm, dtok), (pt_hbm, pt),
    ]):
        moves.append(pltpu.make_async_copy(src, dst, lsem.at[n]))
    doc_in, ga_in, k_in, v_in, ow_in, wo_in, wg_in, wu_in = moves[:8]
    small_in = moves[8:]
    quarter = model // 4
    qw_in = [
        pltpu.make_async_copy(
            qw_hbm.at[pl.ds(n * quarter, quarter)], qw.at[pl.ds(n * quarter, quarter)],
            lsem.at[16 + n],
        )
        for n in range(4)
    ]
    for move in [doc_in, ga_in] + qw_in + small_in + [k_in, v_in]:
        move.start()

    doc_in.wait()
    ga_in.wait()
    x = doc[...].astype(F32)
    scale = lax.rsqrt(jnp.mean(x * x, axis=1, keepdims=True) + 1e-6)
    normed = (x * scale * ga[...]).astype(BF16)
    for move in small_in:
        move.wait()

    docs = dtok[...]

    def fill(step, carry):
        for j in range(16):
            d = step * 16 + j
            carry = jnp.where(docs == d, dq[d], carry)
        return carry

    tokq_row[...] = lax.fori_loop(
        0, ndoc // 16, fill, jnp.zeros((1, total_toks), jnp.int32)
    ).astype(F32)
    lane = iota((1, span), 1)
    half = span // 2
    page = jnp.where(lane < half, p * pages + lane // page_len, partner * pages + (lane - half) // page_len)
    owner = jnp.full((1, span), -1.0, F32)
    left = jnp.zeros((1, span), jnp.int32)
    for s in range(all_pages):
        hit = page == pt[s]
        owner = jnp.where(hit, float(s // max_pages), owner)
        left = jnp.where(hit, ql[s // max_pages] - (s % max_pages) * page_len, left)
    keyq_row[...] = jnp.where(lane % page_len < left, owner, -1.0)

    buckets = bt.shape[1]

    def bias_of(ref, slot):
        for j in range(pages):
            onehot = (ref[j:j + 1, :] == iota((buckets, page_len), 0)).astype(F32)
            part = lax.dot_general(
                bt[...], onehot, (((1,), (0,)), ((), ())),
                precision=lax.Precision.HIGHEST, preferred_element_type=F32,
            )
            at = (slot * pages + j) * page_len
            kbias[:, at:at + page_len] = part

    bias_of(rb, 0)
    pl.semaphore_wait(barrier, npg - 1 + nz - 1)
    pairs = []
    for n, (src, dst) in enumerate([(ck_hbm, kbuf.at[1]), (cv_hbm, vbuf.at[1]), (rb_hbm, rbx)]):
        copy = pltpu.make_async_remote_copy(
            src_ref=src, dst_ref=dst, send_sem=pair_s.at[n], recv_sem=pair_r.at[n],
            device_id=(z, partner), device_id_type=MESH,
        )
        copy.start()
        pairs.append(copy)

    for move in qw_in:
        move.wait()
    q_all[0] = dot(normed, qw[...]).astype(BF16)

    def rows_of(a):
        return pl.ds(pl.multiple_of(a * part, part), part)

    def query_copy(k, a):
        return pltpu.make_async_remote_copy(
            src_ref=q_all.at[0, rows_of(a)], dst_ref=q_all.at[k, rows_of(a)],
            send_sem=q_s.at[a, k], recv_sem=q_r.at[a, k],
            device_id=(z, ((chip + k) % nc) * 2 + core), device_id_type=MESH,
        )

    for a in range(2):
        for k in range(1, nc):
            query_copy(k, a).start()
    for move in (ow_in, wo_in, wg_in, wu_in):
        move.start()

    side = iota((1, 128), 1) // depth
    side_mask = [(side == s).astype(F32).astype(BF16) for s in range(128 // depth)]
    per = 128 // depth

    tall = iota((128, 1), 0) // depth
    tall_mask = [(tall == s).astype(F32) for s in range(per)]

    def split_keys(slot):
        for j in range(pages):
            first = (slot * pages + j) * page_len
            for g in range(width // 128):
                flipped = kbuf[slot, j, :, g * 128:(g + 1) * 128].astype(F32).T
                for s in range(per):
                    kz[g * per + s, :, first:first + page_len] = (flipped * tall_mask[s]).astype(BF16)

    def split_values(slot):
        for j in range(pages):
            first = (slot * pages + j) * page_len
            for h in range(heads):
                g = h // per
                vz[h, first:first + page_len, :] = (
                    vbuf[slot, j, :, g * 128:(g + 1) * 128] * side_mask[h % per]
                )

    k_in.wait()
    split_keys(0)
    v_in.wait()
    split_values(0)
    for copy in pairs:
        copy.wait_recv()
    bias_of(rbx, 1)
    split_keys(1)
    split_values(1)

    spot = iota((1, 128), 1)

    def token_column(row, first, count):
        hit = iota((count, total_toks), 1) == iota((count, total_toks), 0) + first
        return jnp.sum(jnp.where(hit, row, 0.0), axis=1, keepdims=True)

    def lanes_of(g):
        return pl.ds(pl.multiple_of(g * 128, 128), 128)

    def attend(load, store, column):
        far = jnp.where(column == keyq_row[...], 0.0, FAR)

        def four_heads(n, stats):
            some = [n * 4 + j for j in range(4)]
            tiles = [n * (4 // per) + j for j in range(4 // per)]
            rows = [load(g) for g in tiles]
            scores = [
                dot(rows[j // per], kz[h]) + (far + kbias[pl.ds(h, 1), :])
                for j, h in enumerate(some)
            ]
            tops = [jnp.max(score, axis=1, keepdims=True) for score in scores]
            weights = [jnp.exp(score - top) for score, top in zip(scores, tops)]
            totals = [jnp.sum(weight, axis=1, keepdims=True) for weight in weights]
            parts = [dot(weight.astype(BF16), vz[h]) for weight, h in zip(weights, some)]
            for h, top, total in zip(some, tops, totals):
                own = spot % heads == h
                stats = jnp.where(own & (spot < 3 * heads), top, stats)
                stats = jnp.where(own & (spot >= 3 * heads), total, stats)
            for j, g in enumerate(tiles):
                store(g, sum(parts[j * per:(j + 1) * per]).astype(BF16))
            return stats

        stats = lax.fori_loop(
            0, heads // 4, four_heads, jnp.zeros((column.shape[0], 128), F32)
        )
        first, second, third = three_parts(stats)
        turn = (spot // heads) % 3
        packed = jnp.where(turn == 0, first, jnp.where(turn == 1, second, third))
        store(width // 128, jnp.where(spot < 6 * heads, packed, 0.0).astype(BF16))

    def partial_copy(k, a):
        return pltpu.make_async_remote_copy(
            src_ref=ax_out.at[k, rows_of(a)], dst_ref=ax.at[k, rows_of(a)],
            send_sem=a_s.at[a, k], recv_sem=a_r.at[a, k],
            device_id=(z, ((chip - k + nc) % nc) * 2 + core), device_id_type=MESH,
        )

    def own_load(g):
        return q_all[0, :, lanes_of(g)]

    def own_store(g, piece):
        ax[0, :, lanes_of(g)] = piece

    attend(own_load, own_store, token_column(tokq_row[...], p * toks, toks))
    groups = (nc - 1) // group

    def serve(step, carry):
        a = step // groups
        ks = [1 + step % groups * group + n for n in range(group)]
        for k in ks:
            query_copy(k, a).wait_recv()
        column = jnp.concatenate([
            token_column(
                tokq_row[...], (((chip - k + nc) % nc) * 2 + core) * toks + a * part, part
            )
            for k in ks
        ], axis=0)

        def load(g):
            return jnp.concatenate([q_all[k, rows_of(a), lanes_of(g)] for k in ks], axis=0)

        def store(g, piece):
            for n, k in enumerate(ks):
                ax_out[k, rows_of(a), lanes_of(g)] = piece[n * part:(n + 1) * part]

        attend(load, store, column)
        for k in ks:
            partial_copy(k, a).start()
        return carry

    lax.fori_loop(0, 2 * groups, serve, 0)

    lanes = iota((128, width), 0)
    same = lanes % heads == iota((128, width), 1) // depth
    pick_top = (same & (lanes < 3 * heads)).astype(F32).astype(BF16)
    pick_total = (same & (lanes >= 3 * heads) & (lanes < 6 * heads)).astype(F32).astype(BF16)

    def join(a):
        rows = slice(a * part, (a + 1) * part)
        for k in range(1, nc):
            partial_copy(k, a).wait_recv()
        tops = [dot(ax[k, rows, width:], pick_top) for k in range(nc)]
        best = functools.reduce(jnp.maximum, tops)
        total = jnp.zeros((part, width), F32)
        sums = jnp.zeros((part, width), F32)
        for k in range(nc):
            factor = jnp.exp(tops[k] - best)
            total += factor * dot(ax[k, rows, width:], pick_total)
            sums += factor * ax[k, rows, :width].astype(F32)
        return (sums / total).astype(BF16)

    def block_of(k):
        return pl.ds(pl.multiple_of(((z + k) % nz) * block, block), block)

    def scatter_copy(k, a):
        return pltpu.make_async_remote_copy(
            src_ref=rs_out.at[k, rows_of(a)], dst_ref=rs.at[k, rows_of(a)],
            send_sem=r_s.at[a, k], recv_sem=r_r.at[a, k],
            device_id=((z + k) % nz, p), device_id_type=MESH,
        )

    def gather_copy(k, a):
        return pltpu.make_async_remote_copy(
            src_ref=ag.at[0, rows_of(a)], dst_ref=ag.at[k, rows_of(a)],
            send_sem=g_s.at[a, k], recv_sem=g_r.at[a, k],
            device_id=((z + k) % nz, p), device_id_type=MESH,
        )

    order = sorted(range(1, nz), key=lambda k: -min(k, nz - k))
    ow_in.wait()
    halves = []
    for a in range(2):
        rows = slice(a * part, (a + 1) * part)
        context = join(a)
        for k in order:
            rs_out[k, rows, :] = dot(context, ow[:, block_of(k)]).astype(BF16)
            scatter_copy(k, a).start()
        halves.append(doc[rows, block_of(0)].astype(F32) + dot(context, ow[:, block_of(0)]))

    wo_in.wait()
    first, second, third = three_parts(sv[...])
    line = iota((128, model), 0)
    folded = jnp.where(line == 0, first, jnp.where(line == 1, second, jnp.where(line == 2, third, 0.0)))
    for n in range(model // 128):
        svt[n * 128:(n + 1) * 128, :] = folded[:, n * 128:(n + 1) * 128].T.astype(BF16)
    tall_w = jnp.sum(dot(wo[...], svt[...]), axis=1, keepdims=True)
    first, second, third = three_parts(tall_w)
    w2[...] = jnp.where(
        spot == 0, first, jnp.where(spot == 1, second, jnp.where(spot == 2, third, 0.0))
    ).astype(BF16)
    own_docs = token_column(docs.astype(F32), p * toks, toks)
    fin = fz.shape[2]
    member = (own_docs == iota((toks, fin), 1).astype(F32)).astype(F32)
    mine = p * doc_dev + iota((doc_dev, total_toks), 0)
    counts = jnp.sum((docs == mine).astype(F32), axis=1, keepdims=True)

    gain = gf[:, block_of(0)]
    for a in range(2):
        rows = slice(a * part, (a + 1) * part)
        for k in reversed(order):
            scatter_copy(k, a).wait_recv()
            halves[a] += rs[k, rows, :].astype(F32)
        ag[0, rows, :] = (halves[a] * gain).astype(BF16)
        for k in order:
            gather_copy(k, a).start()
    hidden = jnp.concatenate(halves, axis=0)
    tok_score = jnp.sum(hidden * sv[:, block_of(0)], axis=1, keepdims=True)
    squares = jnp.sum(hidden * hidden, axis=1, keepdims=True)
    wg_in.wait()
    wu_in.wait()
    gate = dot(ag[0], wg[block_of(0), :])
    upper = dot(ag[0], wu[block_of(0), :])
    for k in reversed(order):
        gather_copy(k, 0).wait_recv()
        gather_copy(k, 1).wait_recv()
        rows = block_of(nz - k)
        piece = ag[k]
        gate += dot(piece, wg[rows, :])
        upper += dot(piece, wu[rows, :])
        plain = piece.astype(F32) / gf[:, rows]
        squares += jnp.sum(plain * plain, axis=1, keepdims=True)
    scale = lax.rsqrt(squares / model + 1e-6)
    gate = gate * scale
    upper = upper * scale
    middle = (jax.nn.gelu(gate, approximate=True) * upper).astype(BF16)
    tok_score += jnp.sum(dot(middle, w2[...]), axis=1, keepdims=True)

    fz[0] = jnp.broadcast_to(jnp.sum(member * tok_score, axis=0, keepdims=True), fz.shape[1:])

    def z_copy(k):
        return pltpu.make_async_remote_copy(
            src_ref=fz.at[0], dst_ref=fz.at[k], send_sem=z_s.at[k], recv_sem=z_r.at[k],
            device_id=((z + k) % nz, p), device_id_type=MESH,
        )

    def p_copy(k):
        return pltpu.make_async_remote_copy(
            src_ref=fp.at[0], dst_ref=fp.at[k], send_sem=p_s.at[k], recv_sem=p_r.at[k],
            device_id=(z, (p + k) % npg), device_id_type=MESH,
        )

    for k in order:
        z_copy(k).start()
    for k in order:
        z_copy(k).wait_recv()
    fp[0] = jnp.sum(fz[...], axis=0)
    for k in range(1, npg):
        p_copy(k).start()
    for k in range(1, npg):
        p_copy(k).wait_recv()
    pooled = jnp.sum(fp[...], axis=0)
    want = iota((doc_dev, fin), 1) == iota((doc_dev, fin), 0) + p * doc_dev
    picked = jnp.sum(jnp.where(want, pooled[0:1, :], 0.0), axis=1, keepdims=True)
    scores = picked / counts
    eye = iota((doc_dev, doc_dev), 0) == iota((doc_dev, doc_dev), 1)
    out[...] = jnp.sum(jnp.where(eye, scores, 0.0), axis=0, keepdims=True)

    for copy in pairs:
        copy.wait_send()
    for a in range(2):
        for k in range(1, nc):
            query_copy(k, a).wait_send()
            partial_copy(k, a).wait_send()
        for k in range(1, nz):
            scatter_copy(k, a).wait_send()
            gather_copy(k, a).wait_send()
    for k in range(1, nz):
        z_copy(k).wait_send()
    for k in range(1, npg):
        p_copy(k).wait_send()


def per_device(
    nz, npg,
    doc_states, gain_attn, query_weight, cache_keys, cache_values, rel_bucket, bias_table,
    out_weight, gain_ffn, wi_gate, wi_up, wo_ffn, score_vector, query_lengths, doc_query,
    doc_of_token, page_table,
):
    toks, model = doc_states.shape
    width = query_weight.shape[1]
    hidden_units = wi_gate.shape[1]
    heads, buckets = bias_table.shape[1], bias_table.shape[0]
    pages, page_len, _ = cache_keys.shape
    total_toks = doc_of_token.shape[0]
    ndoc = doc_query.shape[0]
    nc = npg // 2
    span = 2 * pages * page_len
    block = model // nz
    fin = max(128, ndoc)
    hbm = pl.BlockSpec(memory_space=pltpu.HBM)
    vmem = pl.BlockSpec(memory_space=pltpu.VMEM)
    dma = pltpu.SemaphoreType.DMA
    result = pl.pallas_call(
        functools.partial(kernel, nz, npg),
        out_shape=jax.ShapeDtypeStruct((1, ndoc // npg), F32),
        in_specs=[hbm] * 17,
        out_specs=vmem,
        scratch_shapes=[
            pltpu.VMEM((1, model), F32),
            pltpu.VMEM((pages, page_len), jnp.int32),
            pltpu.VMEM((heads, buckets), F32),
            pltpu.VMEM((1, model), F32),
            pltpu.VMEM((1, model), F32),
            pltpu.SMEM(query_lengths.shape, jnp.int32),
            pltpu.SMEM(doc_query.shape, jnp.int32),
            pltpu.VMEM((1, total_toks), jnp.int32),
            pltpu.SMEM(page_table.shape, jnp.int32),
            pltpu.VMEM((toks, model), BF16),
            pltpu.VMEM((model, width), BF16),
            pltpu.VMEM((2, pages, page_len, width), BF16),
            pltpu.VMEM((2, pages, page_len, width), BF16),
            pltpu.VMEM((pages, page_len), jnp.int32),
            pltpu.VMEM((width, model), BF16),
            pltpu.VMEM((model, hidden_units), BF16),
            pltpu.VMEM((model, hidden_units), BF16),
            pltpu.VMEM((hidden_units, model), BF16),
            pltpu.VMEM((heads, 128, span), BF16),
            pltpu.VMEM((heads, span, 128), BF16),
            pltpu.VMEM((heads, span), F32),
            pltpu.VMEM((1, total_toks), F32),
            pltpu.VMEM((1, span), F32),
            pltpu.VMEM((nc, toks, width), BF16),
            pltpu.VMEM((nc, toks, width + 128), BF16),
            pltpu.VMEM((nc, toks, width + 128), BF16),
            pltpu.VMEM((nz, toks, block), BF16),
            pltpu.VMEM((nz, toks, block), BF16),
            pltpu.VMEM((nz, toks, block), BF16),
            pltpu.VMEM((nz, 8, fin), F32),
            pltpu.VMEM((npg, 8, fin), F32),
            pltpu.VMEM((model, 128), BF16),
            pltpu.VMEM((hidden_units, 128), BF16),
            dma((20,)), dma((3,)), dma((3,)),
            dma((2, nc)), dma((2, nc)), dma((2, nc)), dma((2, nc)),
            dma((2, nz)), dma((2, nz)), dma((2, nz)), dma((2, nz)), dma((nz,)), dma((nz,)),
            dma((npg,)), dma((npg,)),
        ],
        compiler_params=pltpu.CompilerParams(
            collective_id=0, has_side_effects=True, vmem_limit_bytes=56 * 2**20,
        ),
    )(
        doc_states, gain_attn.reshape(1, -1), query_weight, cache_keys, cache_values, rel_bucket,
        bias_table.T, out_weight, gain_ffn.reshape(1, -1), wi_gate, wi_up, wo_ffn,
        score_vector.reshape(1, -1), query_lengths, doc_query, doc_of_token.reshape(1, -1),
        page_table,
    )
    return result.reshape(-1)


def solution(mesh):
    return jax.shard_map(
        functools.partial(per_device, mesh.shape["head"], mesh.shape["page"]),
        mesh=mesh,
        in_specs=(
            P("page", None),
            P(),
            P(None, "head"),
            P("page", None, "head"),
            P("page", None, "head"),
            P("page", None),
            P(None, "head"),
            P("head", None),
            P(),
            P(None, "head"),
            P(None, "head"),
            P("head", None),
            P(),
            P(),
            P(),
            P(),
            P(),
        ),
        out_specs=P("page"),
        check_vma=False,
    )
```

```python
import functools

import jax
import jax.numpy as jnp
from jax import lax
from jax.experimental import pallas as pl
from jax.experimental.pallas import tpu as pltpu
from jax.sharding import PartitionSpec as P

NQ = 8
FAR = -1e30
MESH = pl.DeviceIdType.MESH
F32 = jnp.float32
BF16 = jnp.bfloat16


def iota(shape, dim):
    return lax.broadcasted_iota(jnp.int32, shape, dim)


def dot(a, b):
    return jnp.dot(a, b, preferred_element_type=F32)


def three_parts(value):
    first = value.astype(BF16).astype(F32)
    second = (value - first).astype(BF16).astype(F32)
    third = (value - first - second).astype(BF16).astype(F32)
    return first, second, third


def kernel(
    nz, npg,
    doc_hbm, ga_hbm, qw_hbm, ck_hbm, cv_hbm, rb_hbm, bt_hbm, ow_hbm, gf_hbm, wg_hbm, wu_hbm,
    wo_hbm, sv_hbm, ql_hbm, dq_hbm, dtok_hbm, pt_hbm,
    out,
    ga, rb, bt, gf, sv, ql, dq, dtok, pt,
    doc, qw, kbuf, vbuf, rbx, ow, wg, wu, wo, kz, vz, kbias, tokq_row, keyq_row,
    q_all, ax_out, ax, rs_out, rs, ag, fz, fp, svt, w2,
    lsem, pair_s, pair_r, q_s, q_r, a_s, a_r, r_s, r_r, g_s, g_r, z_s, z_r, p_s, p_r,
):
    nc = npg // 2
    group = 3 if (nc - 1) % 3 == 0 else 1
    z = lax.axis_index("head")
    p = lax.axis_index("page")
    core = p % 2
    chip = p // 2
    partner = p + 1 - 2 * core
    toks, model = doc.shape
    width = qw.shape[1]
    heads = bt.shape[0]
    depth = width // heads
    pages, page_len = rb.shape
    span = 2 * pages * page_len
    total_toks = dtok.shape[1]
    ndoc = dq.shape[0]
    doc_dev = ndoc // npg
    block = model // nz
    part = toks // 2
    all_pages = pt.shape[0]
    max_pages = all_pages // NQ

    barrier = pltpu.get_barrier_semaphore()
    for k in range(1, npg):
        pl.semaphore_signal(barrier, inc=1, device_id=(z, (p + k) % npg), device_id_type=MESH)
    for k in range(1, nz):
        pl.semaphore_signal(barrier, inc=1, device_id=((z + k) % nz, p), device_id_type=MESH)

    moves = []
    for n, (src, dst) in enumerate([
        (doc_hbm, doc), (ga_hbm, ga),
        (ck_hbm, kbuf.at[0]), (cv_hbm, vbuf.at[0]),
        (ow_hbm, ow), (wo_hbm, wo), (wg_hbm, wg), (wu_hbm, wu),
        (rb_hbm, rb), (bt_hbm, bt), (gf_hbm, gf), (sv_hbm, sv),
        (ql_hbm, ql), (dq_hbm, dq), (dtok_hbm, dtok), (pt_hbm, pt),
    ]):
        moves.append(pltpu.make_async_copy(src, dst, lsem.at[n]))
    doc_in, ga_in, k_in, v_in, ow_in, wo_in, wg_in, wu_in = moves[:8]
    small_in = moves[8:]
    quarter = model // 4
    qw_in = [
        pltpu.make_async_copy(
            qw_hbm.at[pl.ds(n * quarter, quarter)], qw.at[pl.ds(n * quarter, quarter)],
            lsem.at[16 + n],
        )
        for n in range(4)
    ]
    for move in [doc_in, ga_in] + qw_in + small_in + [k_in, v_in]:
        move.start()

    doc_in.wait()
    ga_in.wait()
    x = doc[...].astype(F32)
    scale = lax.rsqrt(jnp.mean(x * x, axis=1, keepdims=True) + 1e-6)
    normed = (x * scale * ga[...]).astype(BF16)
    for move in small_in:
        move.wait()

    docs = dtok[...]

    def fill(step, carry):
        for j in range(16):
            d = step * 16 + j
            carry = jnp.where(docs == d, dq[d], carry)
        return carry

    tokq_row[...] = lax.fori_loop(
        0, ndoc // 16, fill, jnp.zeros((1, total_toks), jnp.int32)
    ).astype(F32)
    lane = iota((1, span), 1)
    half = span // 2
    page = jnp.where(lane < half, p * pages + lane // page_len, partner * pages + (lane - half) // page_len)
    owner = jnp.full((1, span), -1.0, F32)
    left = jnp.zeros((1, span), jnp.int32)
    for s in range(all_pages):
        hit = page == pt[s]
        owner = jnp.where(hit, float(s // max_pages), owner)
        left = jnp.where(hit, ql[s // max_pages] - (s % max_pages) * page_len, left)
    keyq_row[...] = jnp.where(lane % page_len < left, owner, -1.0)

    buckets = bt.shape[1]

    def bias_of(ref, slot):
        for j in range(pages):
            onehot = (ref[j:j + 1, :] == iota((buckets, page_len), 0)).astype(F32)
            part = lax.dot_general(
                bt[...], onehot, (((1,), (0,)), ((), ())),
                precision=lax.Precision.HIGHEST, preferred_element_type=F32,
            )
            at = (slot * pages + j) * page_len
            kbias[:, at:at + page_len] = part

    bias_of(rb, 0)
    pl.semaphore_wait(barrier, npg - 1 + nz - 1)
    pairs = []
    for n, (src, dst) in enumerate([(ck_hbm, kbuf.at[1]), (cv_hbm, vbuf.at[1]), (rb_hbm, rbx)]):
        copy = pltpu.make_async_remote_copy(
            src_ref=src, dst_ref=dst, send_sem=pair_s.at[n], recv_sem=pair_r.at[n],
            device_id=(z, partner), device_id_type=MESH,
        )
        copy.start()
        pairs.append(copy)

    for move in qw_in:
        move.wait()
    q_all[0] = dot(normed, qw[...]).astype(BF16)

    def rows_of(a):
        return pl.ds(pl.multiple_of(a * part, part), part)

    def query_copy(k, a):
        return pltpu.make_async_remote_copy(
            src_ref=q_all.at[0, rows_of(a)], dst_ref=q_all.at[k, rows_of(a)],
            send_sem=q_s.at[a, k], recv_sem=q_r.at[a, k],
            device_id=(z, ((chip + k) % nc) * 2 + core), device_id_type=MESH,
        )

    for a in range(2):
        for k in range(1, nc):
            query_copy(k, a).start()
    for move in (ow_in, wo_in, wg_in, wu_in):
        move.start()

    side = iota((1, 128), 1) // depth
    side_mask = [(side == s).astype(F32).astype(BF16) for s in range(128 // depth)]
    per = 128 // depth

    tall = iota((128, 1), 0) // depth
    tall_mask = [(tall == s).astype(F32) for s in range(per)]

    def split_keys(slot):
        for j in range(pages):
            first = (slot * pages + j) * page_len
            for g in range(width // 128):
                flipped = kbuf[slot, j, :, g * 128:(g + 1) * 128].astype(F32).T
                for s in range(per):
                    kz[g * per + s, :, first:first + page_len] = (flipped * tall_mask[s]).astype(BF16)

    def split_values(slot):
        for j in range(pages):
            first = (slot * pages + j) * page_len
            for h in range(heads):
                g = h // per
                vz[h, first:first + page_len, :] = (
                    vbuf[slot, j, :, g * 128:(g + 1) * 128] * side_mask[h % per]
                )

    k_in.wait()
    split_keys(0)
    v_in.wait()
    split_values(0)
    for copy in pairs:
        copy.wait_recv()
    bias_of(rbx, 1)
    split_keys(1)
    split_values(1)

    spot = iota((1, 128), 1)

    def token_column(row, first, count):
        hit = iota((count, total_toks), 1) == iota((count, total_toks), 0) + first
        return jnp.sum(jnp.where(hit, row, 0.0), axis=1, keepdims=True)

    def lanes_of(g):
        return pl.ds(pl.multiple_of(g * 128, 128), 128)

    def attend(load, store, column):
        far = jnp.where(column == keyq_row[...], 0.0, FAR)

        def four_heads(n, stats):
            some = [n * 4 + j for j in range(4)]
            tiles = [n * (4 // per) + j for j in range(4 // per)]
            rows = [load(g) for g in tiles]
            scores = [
                dot(rows[j // per], kz[h]) + (far + kbias[pl.ds(h, 1), :])
                for j, h in enumerate(some)
            ]
            tops = [jnp.max(score, axis=1, keepdims=True) for score in scores]
            weights = [jnp.exp(score - top) for score, top in zip(scores, tops)]
            totals = [jnp.sum(weight, axis=1, keepdims=True) for weight in weights]
            parts = [dot(weight.astype(BF16), vz[h]) for weight, h in zip(weights, some)]
            for h, top, total in zip(some, tops, totals):
                own = spot % heads == h
                stats = jnp.where(own & (spot < 3 * heads), top, stats)
                stats = jnp.where(own & (spot >= 3 * heads), total, stats)
            for j, g in enumerate(tiles):
                store(g, sum(parts[j * per:(j + 1) * per]).astype(BF16))
            return stats

        stats = jnp.zeros((column.shape[0], 128), F32)
        for n in range(heads // 4):
            stats = four_heads(n, stats)
        first, second, third = three_parts(stats)
        turn = (spot // heads) % 3
        packed = jnp.where(turn == 0, first, jnp.where(turn == 1, second, third))
        store(width // 128, jnp.where(spot < 6 * heads, packed, 0.0).astype(BF16))

    def partial_copy(k, a):
        return pltpu.make_async_remote_copy(
            src_ref=ax_out.at[k, rows_of(a)], dst_ref=ax.at[k, rows_of(a)],
            send_sem=a_s.at[a, k], recv_sem=a_r.at[a, k],
            device_id=(z, ((chip - k + nc) % nc) * 2 + core), device_id_type=MESH,
        )

    def own_load(g):
        return q_all[0, :, lanes_of(g)]

    def own_store(g, piece):
        ax[0, :, lanes_of(g)] = piece

    attend(own_load, own_store, token_column(tokq_row[...], p * toks, toks))
    groups = (nc - 1) // group

    def serve(step, carry):
        a = step // groups
        ks = [1 + step % groups * group + n for n in range(group)]
        for k in ks:
            query_copy(k, a).wait_recv()
        column = jnp.concatenate([
            token_column(
                tokq_row[...], (((chip - k + nc) % nc) * 2 + core) * toks + a * part, part
            )
            for k in ks
        ], axis=0)

        def load(g):
            return jnp.concatenate([q_all[k, rows_of(a), lanes_of(g)] for k in ks], axis=0)

        def store(g, piece):
            for n, k in enumerate(ks):
                ax_out[k, rows_of(a), lanes_of(g)] = piece[n * part:(n + 1) * part]

        attend(load, store, column)
        for k in ks:
            partial_copy(k, a).start()
        return carry

    if groups == 1:
        for step in range(2):
            serve(step, 0)
    else:
        lax.fori_loop(0, 2 * groups, serve, 0)

    lanes = iota((128, width), 0)
    same = lanes % heads == iota((128, width), 1) // depth
    pick_top = (same & (lanes < 3 * heads)).astype(F32).astype(BF16)
    pick_total = (same & (lanes >= 3 * heads) & (lanes < 6 * heads)).astype(F32).astype(BF16)

    def join(a):
        rows = slice(a * part, (a + 1) * part)
        for k in range(1, nc):
            partial_copy(k, a).wait_recv()
        tops = [dot(ax[k, rows, width:], pick_top) for k in range(nc)]
        best = functools.reduce(jnp.maximum, tops)
        total = jnp.zeros((part, width), F32)
        sums = jnp.zeros((part, width), F32)
        for k in range(nc):
            factor = jnp.exp(tops[k] - best)
            total += factor * dot(ax[k, rows, width:], pick_total)
            sums += factor * ax[k, rows, :width].astype(F32)
        return (sums / total).astype(BF16)

    def block_of(k):
        return pl.ds(pl.multiple_of(((z + k) % nz) * block, block), block)

    def scatter_copy(k, a):
        return pltpu.make_async_remote_copy(
            src_ref=rs_out.at[k, rows_of(a)], dst_ref=rs.at[k, rows_of(a)],
            send_sem=r_s.at[a, k], recv_sem=r_r.at[a, k],
            device_id=((z + k) % nz, p), device_id_type=MESH,
        )

    def gather_copy(k, a):
        return pltpu.make_async_remote_copy(
            src_ref=ag.at[0, rows_of(a)], dst_ref=ag.at[k, rows_of(a)],
            send_sem=g_s.at[a, k], recv_sem=g_r.at[a, k],
            device_id=((z + k) % nz, p), device_id_type=MESH,
        )

    order = sorted(range(1, nz), key=lambda k: -min(k, nz - k))
    ow_in.wait()
    halves = []
    for a in range(2):
        rows = slice(a * part, (a + 1) * part)
        context = join(a)
        for k in order:
            rs_out[k, rows, :] = dot(context, ow[:, block_of(k)]).astype(BF16)
            scatter_copy(k, a).start()
        halves.append(doc[rows, block_of(0)].astype(F32) + dot(context, ow[:, block_of(0)]))

    wo_in.wait()
    first, second, third = three_parts(sv[...])
    line = iota((128, model), 0)
    folded = jnp.where(line == 0, first, jnp.where(line == 1, second, jnp.where(line == 2, third, 0.0)))
    for n in range(model // 128):
        svt[n * 128:(n + 1) * 128, :] = folded[:, n * 128:(n + 1) * 128].T.astype(BF16)
    tall_w = jnp.sum(dot(wo[...], svt[...]), axis=1, keepdims=True)
    first, second, third = three_parts(tall_w)
    w2[...] = jnp.where(
        spot == 0, first, jnp.where(spot == 1, second, jnp.where(spot == 2, third, 0.0))
    ).astype(BF16)
    own_docs = token_column(docs.astype(F32), p * toks, toks)
    fin = fz.shape[2]
    member = (own_docs == iota((toks, fin), 1).astype(F32)).astype(F32)
    mine = p * doc_dev + iota((doc_dev, total_toks), 0)
    counts = jnp.sum((docs == mine).astype(F32), axis=1, keepdims=True)

    gain = gf[:, block_of(0)]
    for a in range(2):
        rows = slice(a * part, (a + 1) * part)
        for k in reversed(order):
            scatter_copy(k, a).wait_recv()
            halves[a] += rs[k, rows, :].astype(F32)
        ag[0, rows, :] = (halves[a] * gain).astype(BF16)
        for k in order:
            gather_copy(k, a).start()
    hidden = jnp.concatenate(halves, axis=0)
    tok_score = jnp.sum(hidden * sv[:, block_of(0)], axis=1, keepdims=True)
    squares = jnp.sum(hidden * hidden, axis=1, keepdims=True)
    wg_in.wait()
    wu_in.wait()
    gate = dot(ag[0], wg[block_of(0), :])
    upper = dot(ag[0], wu[block_of(0), :])
    for k in reversed(order):
        gather_copy(k, 0).wait_recv()
        gather_copy(k, 1).wait_recv()
        rows = block_of(nz - k)
        piece = ag[k]
        gate += dot(piece, wg[rows, :])
        upper += dot(piece, wu[rows, :])
        plain = piece.astype(F32) / gf[:, rows]
        squares += jnp.sum(plain * plain, axis=1, keepdims=True)
    scale = lax.rsqrt(squares / model + 1e-6)
    gate = gate * scale
    upper = upper * scale
    middle = (jax.nn.gelu(gate, approximate=True) * upper).astype(BF16)
    tok_score += jnp.sum(dot(middle, w2[...]), axis=1, keepdims=True)

    fz[0] = jnp.broadcast_to(jnp.sum(member * tok_score, axis=0, keepdims=True), fz.shape[1:])

    def z_copy(k):
        return pltpu.make_async_remote_copy(
            src_ref=fz.at[0], dst_ref=fz.at[k], send_sem=z_s.at[k], recv_sem=z_r.at[k],
            device_id=((z + k) % nz, p), device_id_type=MESH,
        )

    def p_copy(k):
        return pltpu.make_async_remote_copy(
            src_ref=fp.at[0], dst_ref=fp.at[k], send_sem=p_s.at[k], recv_sem=p_r.at[k],
            device_id=(z, (p + k) % npg), device_id_type=MESH,
        )

    for k in order:
        z_copy(k).start()
    for k in order:
        z_copy(k).wait_recv()
    fp[0] = jnp.sum(fz[...], axis=0)
    for k in range(1, npg):
        p_copy(k).start()
    for k in range(1, npg):
        p_copy(k).wait_recv()
    pooled = jnp.sum(fp[...], axis=0)
    want = iota((doc_dev, fin), 1) == iota((doc_dev, fin), 0) + p * doc_dev
    picked = jnp.sum(jnp.where(want, pooled[0:1, :], 0.0), axis=1, keepdims=True)
    scores = picked / counts
    eye = iota((doc_dev, doc_dev), 0) == iota((doc_dev, doc_dev), 1)
    out[...] = jnp.sum(jnp.where(eye, scores, 0.0), axis=0, keepdims=True)

    for copy in pairs:
        copy.wait_send()
    for a in range(2):
        for k in range(1, nc):
            query_copy(k, a).wait_send()
            partial_copy(k, a).wait_send()
        for k in range(1, nz):
            scatter_copy(k, a).wait_send()
            gather_copy(k, a).wait_send()
    for k in range(1, nz):
        z_copy(k).wait_send()
    for k in range(1, npg):
        p_copy(k).wait_send()


def per_device(
    nz, npg,
    doc_states, gain_attn, query_weight, cache_keys, cache_values, rel_bucket, bias_table,
    out_weight, gain_ffn, wi_gate, wi_up, wo_ffn, score_vector, query_lengths, doc_query,
    doc_of_token, page_table,
):
    toks, model = doc_states.shape
    width = query_weight.shape[1]
    hidden_units = wi_gate.shape[1]
    heads, buckets = bias_table.shape[1], bias_table.shape[0]
    pages, page_len, _ = cache_keys.shape
    total_toks = doc_of_token.shape[0]
    ndoc = doc_query.shape[0]
    nc = npg // 2
    span = 2 * pages * page_len
    block = model // nz
    fin = max(128, ndoc)
    hbm = pl.BlockSpec(memory_space=pltpu.HBM)
    vmem = pl.BlockSpec(memory_space=pltpu.VMEM)
    dma = pltpu.SemaphoreType.DMA
    result = pl.pallas_call(
        functools.partial(kernel, nz, npg),
        out_shape=jax.ShapeDtypeStruct((1, ndoc // npg), F32),
        in_specs=[hbm] * 17,
        out_specs=vmem,
        scratch_shapes=[
            pltpu.VMEM((1, model), F32),
            pltpu.VMEM((pages, page_len), jnp.int32),
            pltpu.VMEM((heads, buckets), F32),
            pltpu.VMEM((1, model), F32),
            pltpu.VMEM((1, model), F32),
            pltpu.SMEM(query_lengths.shape, jnp.int32),
            pltpu.SMEM(doc_query.shape, jnp.int32),
            pltpu.VMEM((1, total_toks), jnp.int32),
            pltpu.SMEM(page_table.shape, jnp.int32),
            pltpu.VMEM((toks, model), BF16),
            pltpu.VMEM((model, width), BF16),
            pltpu.VMEM((2, pages, page_len, width), BF16),
            pltpu.VMEM((2, pages, page_len, width), BF16),
            pltpu.VMEM((pages, page_len), jnp.int32),
            pltpu.VMEM((width, model), BF16),
            pltpu.VMEM((model, hidden_units), BF16),
            pltpu.VMEM((model, hidden_units), BF16),
            pltpu.VMEM((hidden_units, model), BF16),
            pltpu.VMEM((heads, 128, span), BF16),
            pltpu.VMEM((heads, span, 128), BF16),
            pltpu.VMEM((heads, span), F32),
            pltpu.VMEM((1, total_toks), F32),
            pltpu.VMEM((1, span), F32),
            pltpu.VMEM((nc, toks, width), BF16),
            pltpu.VMEM((nc, toks, width + 128), BF16),
            pltpu.VMEM((nc, toks, width + 128), BF16),
            pltpu.VMEM((nz, toks, block), BF16),
            pltpu.VMEM((nz, toks, block), BF16),
            pltpu.VMEM((nz, toks, block), BF16),
            pltpu.VMEM((nz, 8, fin), F32),
            pltpu.VMEM((npg, 8, fin), F32),
            pltpu.VMEM((model, 128), BF16),
            pltpu.VMEM((hidden_units, 128), BF16),
            dma((20,)), dma((3,)), dma((3,)),
            dma((2, nc)), dma((2, nc)), dma((2, nc)), dma((2, nc)),
            dma((2, nz)), dma((2, nz)), dma((2, nz)), dma((2, nz)), dma((nz,)), dma((nz,)),
            dma((npg,)), dma((npg,)),
        ],
        compiler_params=pltpu.CompilerParams(
            collective_id=0, has_side_effects=True, vmem_limit_bytes=56 * 2**20,
        ),
    )(
        doc_states, gain_attn.reshape(1, -1), query_weight, cache_keys, cache_values, rel_bucket,
        bias_table.T, out_weight, gain_ffn.reshape(1, -1), wi_gate, wi_up, wo_ffn,
        score_vector.reshape(1, -1), query_lengths, doc_query, doc_of_token.reshape(1, -1),
        page_table,
    )
    return result.reshape(-1)


def solution(mesh):
    return jax.shard_map(
        functools.partial(per_device, mesh.shape["head"], mesh.shape["page"]),
        mesh=mesh,
        in_specs=(
            P("page", None),
            P(),
            P(None, "head"),
            P("page", None, "head"),
            P("page", None, "head"),
            P("page", None),
            P(None, "head"),
            P("head", None),
            P(),
            P(None, "head"),
            P(None, "head"),
            P("head", None),
            P(),
            P(),
            P(),
            P(),
            P(),
        ),
        out_specs=P("page"),
        check_vma=False,
    )
```
